32 devices in a mesh: lon: 8 (over y, x, core), lat: 4 (over z).
Axes of the slice: x: 2, y: 2, z: 4, core: 2. Of those that a mesh axis runs over, the one named last changes fastest.
Arguments:
- thermal_anomaly: float32 [46, 32, 1024], P(None, 'lat', 'lon'), may hold values from -6 to 6
- saltiness_anomaly: float32 [46, 32, 1024], P(None, 'lat', 'lon'), may hold values from -6 to 6
- zonal_volume_flux: float32 [46, 32, 1024], P(None, 'lat', 'lon'), may hold values from -0.2 to 0.2
- meridional_volume_flux: float32 [46, 32, 1024], P(None, 'lat', 'lon'), may hold values from -0.2 to 0.2
- vertical_diffusion_factor: float32 [46, 32, 1024], P(None, 'lat', 'lon'), may hold values from 0.05 to 5
- friction_factor: float32 [46, 32, 1024], P(None, 'lat', 'lon'), may hold values from 0.1 to 3
- seawater_indicator: int32 [32, 1024], P('lat', 'lon'), may hold values 0 or 1
- water_layer_depth: int32 [32, 1024], P('lat', 'lon'), may hold values from 1 to 46
Outputs:
- temperature_next: float32 [46, 32, 1024], P(None, 'lat', 'lon')
- salinity_next: float32 [46, 32, 1024], P(None, 'lat', 'lon')
The draws below stay inside these ranges and needn't reach their ends.
All inputs are finite; a program needn't handle non-finite values. No bound on the sum of `seawater_indicator` on one device may be relied on, other than what follows from the above.
Results may differ from the reference program's by a relative error of at most 0.00002.
Values sent between devices are 32-bit elements; how exact they have to be, the bound alone decides.
A program may use at most 64 MiB of HBM per device.

```python
import math
import jax
import jax.numpy as jnp

DEPTH_LAYERS = 46
SPLIT_PASSES = 4
MERIDIAN_NUMBER = 1024
PARALLEL_NUMBER = 32


def plant(result, key, least, largest):
    longest = result.shape.index(max(result.shape))
    spots = []
    for shift in (0, 1):
        where = [jax.random.randint(jax.random.fold_in(key, axis), (), 0, length) for axis, length in enumerate(result.shape)]
        where[longest] = (where[longest] + shift) % result.shape[longest]
        spots.append(tuple(where))
    return result.at[spots[0]].set(least).at[spots[1]].set(largest)


def steps_of(rng, extent, cuts, low, largest):
    def one(position, parts):
        draws = jax.random.uniform(jax.random.fold_in(jax.random.fold_in(rng, 6), position), (parts,), jnp.float32, low / len(cuts), largest / len(cuts))
        return jnp.repeat(jnp.exp(draws), extent[position] // parts).reshape((-1,) + (1,) * (len(extent) - position - 1))

    gain = one(*cuts[0])
    for cut in cuts[1:]:
        gain = gain * one(*cut)
    return gain


def scatter_about(rng, extent, scale, most, pieces=(), kind=jnp.bfloat16):
    entries = jax.random.normal(rng, extent, jnp.float32) * scale
    if len(pieces) > 0:
        entries = steps_of(rng, extent, pieces, -0.22, 0.18) * entries
    return jnp.clip(entries, min=-most, max=most).astype(kind)


def setup_inputs(seed: int = 0) -> dict:
    arg_keys = jax.random.split(jax.random.key(seed), 9)
    thermal_anomaly = scatter_about(arg_keys[0], (DEPTH_LAYERS, PARALLEL_NUMBER, MERIDIAN_NUMBER), 1.0, 6.0, ((1, 4), (2, 8)), jnp.float32)
    saltiness_anomaly = scatter_about(arg_keys[1], (DEPTH_LAYERS, PARALLEL_NUMBER, MERIDIAN_NUMBER), 1.0, 6.0, ((1, 4), (2, 8)), jnp.float32)
    zonal_volume_flux = jnp.clip(jax.random.uniform(arg_keys[2], (DEPTH_LAYERS, PARALLEL_NUMBER, MERIDIAN_NUMBER), jnp.float32, -0.2, 0.2) * steps_of(arg_keys[2], (DEPTH_LAYERS, PARALLEL_NUMBER, MERIDIAN_NUMBER), ((1, 4), (2, 8)), -0.4, 0.0), -0.2, 0.2)
    meridional_volume_flux = jnp.clip(jax.random.uniform(arg_keys[3], (DEPTH_LAYERS, PARALLEL_NUMBER, MERIDIAN_NUMBER), jnp.float32, -0.2, 0.2) * steps_of(arg_keys[3], (DEPTH_LAYERS, PARALLEL_NUMBER, MERIDIAN_NUMBER), ((1, 4), (2, 8)), -0.4, 0.0), -0.2, 0.2)
    vertical_diffusion_factor = jnp.clip(jnp.exp(math.log(5.0) - 4.6051702 * jax.random.uniform(arg_keys[4], (DEPTH_LAYERS, PARALLEL_NUMBER, MERIDIAN_NUMBER), jnp.float32) ** steps_of(arg_keys[4], (DEPTH_LAYERS, PARALLEL_NUMBER, MERIDIAN_NUMBER), ((1, 4), (2, 8)), -0.2, 0.2)), 0.05, 5.0)
    friction_factor = jnp.clip(jnp.exp(math.log(3.0) - 3.4011974 * jax.random.uniform(arg_keys[5], (DEPTH_LAYERS, PARALLEL_NUMBER, MERIDIAN_NUMBER), jnp.float32) ** steps_of(arg_keys[5], (DEPTH_LAYERS, PARALLEL_NUMBER, MERIDIAN_NUMBER), ((1, 4), (2, 8)), -0.2, 0.2)), 0.1, 3.0)
    seawater_indicator = plant((jax.random.randint(arg_keys[6], (PARALLEL_NUMBER, MERIDIAN_NUMBER), 0, 5) < 4).astype(jnp.int32), jax.random.fold_in(arg_keys[6], 1), 0, 1)
    water_layer_depth = plant(jax.random.randint(arg_keys[7], (PARALLEL_NUMBER, MERIDIAN_NUMBER), 1, DEPTH_LAYERS + 1), jax.random.fold_in(arg_keys[7], 1), 1, DEPTH_LAYERS).astype(jnp.int32)
    return dict(thermal_anomaly=thermal_anomaly, saltiness_anomaly=saltiness_anomaly, zonal_volume_flux=zonal_volume_flux, meridional_volume_flux=meridional_volume_flux, vertical_diffusion_factor=vertical_diffusion_factor, friction_factor=friction_factor, seawater_indicator=seawater_indicator, water_layer_depth=water_layer_depth)


DIFFUSE = 0.05


def shifted_scalar(stacked):
    west_side = jnp.roll(stacked, 1, axis=-1)
    east_side = jnp.roll(stacked, -1, axis=-1)
    south_side = jnp.concatenate([jnp.zeros_like(stacked[..., :1, :]), stacked[..., :-1, :]], axis=-2)
    north_side = jnp.concatenate([stacked[..., 1:, :], stacked[..., -1:, ::-1]], axis=-2)
    return west_side, east_side, south_side, north_side


def tridiagonal(lower_band, main_band, upper_band, right_side):
    water_layer_number = main_band.shape[0]
    sweep_ratio = upper_band[0] / main_band[0]
    sweep_value = right_side[:, 0] / main_band[0]
    ratio_list = [sweep_ratio]
    value_list = [sweep_value]
    for level_index in range(1, water_layer_number):
        pivot_value = main_band[level_index] - lower_band[level_index] * sweep_ratio
        sweep_ratio = upper_band[level_index] / pivot_value
        sweep_value = (right_side[:, level_index] - lower_band[level_index] * sweep_value) / pivot_value
        ratio_list.append(sweep_ratio)
        value_list.append(sweep_value)
    solved_level = value_list[-1]
    solved_rows = [solved_level]
    for level_index in range(water_layer_number - 2, -1, -1):
        solved_level = value_list[level_index] - ratio_list[level_index] * solved_level
        solved_rows.append(solved_level)
    return jnp.stack(solved_rows[::-1], axis=1)


def march_scalars(thermal_anomaly, saltiness_anomaly, zonal_volume_flux, meridional_volume_flux, vertical_diffusion_factor, friction_factor, seawater_indicator, water_layer_depth, neighbour_sites, hinge_parallels, advection_passes):
    water_layer_number = thermal_anomaly.shape[0]
    depth_index = jnp.arange(water_layer_number, dtype=jnp.int32)[:, None, None]
    seawater_sites = jnp.where((seawater_indicator[None] == 1) & (depth_index < water_layer_depth[None]), 1.0, 0.0).astype(jnp.float32)
    damping = 1.0 + friction_factor
    east_flow = zonal_volume_flux / damping
    north_flow = meridional_volume_flux / damping
    west_side, east_side, south_side, north_side = neighbour_sites(jnp.stack([east_flow, north_flow, seawater_sites]))
    open_east = seawater_sites * east_side[2]
    open_west = west_side[2] * seawater_sites
    open_north = seawater_sites * north_side[2]
    open_south = south_side[2] * seawater_sites
    flow_west_face = west_side[0]
    flow_south_face = south_side[1]
    flow_north_face = jnp.where(hinge_parallels, 0.5 * (north_flow - north_side[1]), north_flow)
    scalar_quantities = jnp.stack([thermal_anomaly, saltiness_anomaly]) * seawater_sites
    for substep in range(advection_passes):
        west_tr, east_tr, south_tr, north_tr = neighbour_sites(scalar_quantities)
        flux_east = open_east * (jnp.maximum(east_flow, 0.0) * scalar_quantities + jnp.minimum(east_flow, 0.0) * east_tr - DIFFUSE * (east_tr - scalar_quantities))
        flux_west = open_west * (jnp.maximum(flow_west_face, 0.0) * west_tr + jnp.minimum(flow_west_face, 0.0) * scalar_quantities - DIFFUSE * (scalar_quantities - west_tr))
        flux_north = open_north * (jnp.maximum(flow_north_face, 0.0) * scalar_quantities + jnp.minimum(flow_north_face, 0.0) * north_tr - DIFFUSE * (north_tr - scalar_quantities))
        flux_south = open_south * (jnp.maximum(flow_south_face, 0.0) * south_tr + jnp.minimum(flow_south_face, 0.0) * scalar_quantities - DIFFUSE * (scalar_quantities - south_tr))
        scalar_quantities = scalar_quantities - (flux_east - flux_west + flux_north - flux_south)
    divergence = open_east * east_flow - open_west * flow_west_face + open_north * flow_north_face - open_south * flow_south_face
    deeper_sum = jnp.cumsum(divergence[::-1], axis=0)[::-1]
    zero_face = jnp.zeros_like(deeper_sum[:1])
    transport = -float(advection_passes) * jnp.concatenate([zero_face, deeper_sum[1:], zero_face], axis=0)
    mixing_faces = jnp.concatenate([zero_face, vertical_diffusion_factor[:-1] * seawater_sites[:-1] * seawater_sites[1:], zero_face], axis=0)
    main_band = 1.0 - jnp.minimum(transport[1:], 0.0) + mixing_faces[1:] + jnp.maximum(transport[:-1], 0.0) + mixing_faces[:-1]
    upper_band = -(jnp.maximum(transport[1:], 0.0) + mixing_faces[1:])
    lower_band = jnp.minimum(transport[:-1], 0.0) - mixing_faces[:-1]
    solved = tridiagonal(lower_band, main_band, upper_band, scalar_quantities)
    return solved[0], solved[1]


def reference(thermal_anomaly, saltiness_anomaly, zonal_volume_flux, meridional_volume_flux, vertical_diffusion_factor, friction_factor, seawater_indicator, water_layer_depth):
    parallel_number = thermal_anomaly.shape[1]
    hinge_parallels = (jnp.arange(parallel_number) == parallel_number - 1)[None, :, None]
    return march_scalars(thermal_anomaly, saltiness_anomaly, zonal_volume_flux, meridional_volume_flux, vertical_diffusion_factor, friction_factor, seawater_indicator, water_layer_depth, shifted_scalar, hinge_parallels, SPLIT_PASSES)
```

```python
import functools

import jax
import jax.numpy as jnp
from jax import lax
from jax.experimental import pallas as pl
from jax.experimental.pallas import tpu as pltpu
from jax.sharding import PartitionSpec as P

PASSES = 4
DIFFUSE = 0.05
MESH = pl.DeviceIdType.MESH
F32 = jnp.float32


def tracer_kernel(
    nlon, nlat, depth,
    th, sa, zo, me, vd, fr, ind, dep, out_t, out_s,
    fields, maps, c, acc, ef, nf, coef, dv, upp, low, ip, mm, qq, res,
    lon_out, lon_w, lon_e, n_out, s_out, n_in, s_in,
    in_sem, send_sem, recv_sem, out_sem,
):
    padded = -(-depth // 8) * 8
    rows = 8 * depth
    lon = lax.axis_index("lon")
    lat = lax.axis_index("lat")
    is_top = lat == nlat - 1
    east = lax.rem(lon + 1, nlon)
    west = lax.rem(lon + nlon - 1, nlon)
    mirror = nlon - 1 - lon

    barrier = pltpu.get_barrier_semaphore()

    def greet(i, j):
        pl.semaphore_signal(barrier, inc=1, device_id={"lon": i, "lat": j}, device_id_type=MESH)

    greet(east, lat)
    greet(west, lat)

    @pl.when(is_top)
    def _():
        greet(mirror, lat)

    @pl.when(jnp.logical_not(is_top))
    def _():
        greet(lon, lat + 1)

    @pl.when(lat > 0)
    def _():
        greet(lon, lat - 1)

    loads = [
        pltpu.make_async_copy(ind, maps.at[0], in_sem.at[0]),
        pltpu.make_async_copy(dep, maps.at[1], in_sem.at[1]),
    ]
    for f, ref in enumerate((fr, zo, me, th, sa, vd)):
        loads.append(pltpu.make_async_copy(ref, fields.at[f], in_sem.at[2 + f]))
    for load in loads:
        load.start()

    lane = lax.broadcasted_iota(jnp.int32, (8, 128), 1)
    sub = lax.broadcasted_iota(jnp.int32, (8, 128), 0)
    pair = lax.shift_right_logical(lane, 1)
    even = (lane & 1) == 0
    first, last = lane == 0, lane == 127
    bottom_row, top_row = sub == 0, sub == 7
    hinge = jnp.logical_and(top_row, is_top)
    turned = jnp.where(is_top, 127 - lane, lane)
    zero = jnp.zeros((8, 128), F32)

    def at(k):
        return pl.ds(pl.multiple_of(k * 8, 8), 8)

    def loop(count, body, init):
        return lax.fori_loop(0, count, body, init, unroll=count)

    def pack(x, k, packed):
        return jnp.where(pair == k, pltpu.roll(x, 2 * k + 1, 1), packed)

    def merge(from_west, from_east):
        return jnp.where(even, pltpu.roll(from_east, 127, 1), pltpu.roll(from_west, 1, 1))

    def unpack(merged, k):
        return pltpu.roll(merged, 127 - 2 * k, 1)

    def spread(ref, r, row):
        return jnp.broadcast_to(ref[r, pl.ds(row, 1), :], (8, 128))

    def turn(x):
        return jnp.take_along_axis(x, turned, axis=1, mode="promise_in_bounds")

    def stage_rows(r, ref, base, slot):
        for j in range(padded // 8):
            place = pl.ds(8 + slot * padded + 8 * j, 8)
            s_out[r, place, :] = ref[pl.ds(base + 64 * j, 8, stride=8), :]
            n_out[r, place, :] = turn(ref[pl.ds(base + 64 * j + 7, 8, stride=8), :])

    def remote(src, dst, r, way, i, j):
        return pltpu.make_async_remote_copy(
            src_ref=src, dst_ref=dst, send_sem=send_sem.at[r, way], recv_sem=recv_sem.at[r, way],
            device_id={"lon": i, "lat": j}, device_id_type=MESH,
        )

    def span(r):
        if r == 0:
            return pl.ds(0, 24), pl.ds(0, 8 + 3 * padded)
        return pl.ds(0, 16), pl.ds(8, 2 * padded)

    def to_east(r):
        s = span(r)[0]
        return remote(lon_out.at[r, s], lon_w.at[r, s], r, 0, east, lat)

    def to_west(r):
        s = span(r)[0]
        return remote(lon_out.at[r, s], lon_e.at[r, s], r, 1, west, lat)

    def to_north(r):
        s = span(r)[1]
        return remote(n_out.at[r, s], s_in.at[r, s], r, 3, lon, lat + 1)

    def to_mirror(r):
        s = span(r)[1]
        return pltpu.make_async_remote_copy(
            src_ref=n_out.at[r, s], dst_ref=n_in.at[r, s], send_sem=send_sem.at[r, 3],
            recv_sem=recv_sem.at[r, 2], device_id={"lon": mirror, "lat": lat}, device_id_type=MESH,
        )

    def to_south(r):
        s = span(r)[1]
        return remote(s_out.at[r, s], n_in.at[r, s], r, 2, lon, lat - 1)

    def send_lat(r):
        @pl.when(is_top)
        def _():
            to_mirror(r).start()

        @pl.when(jnp.logical_not(is_top))
        def _():
            to_north(r).start()

        @pl.when(lat > 0)
        def _():
            to_south(r).start()

    def send_lon(r):
        to_east(r).start()
        to_west(r).start()

    def wait_recv(r):
        to_east(r).wait_recv()
        to_west(r).wait_recv()
        to_south(r).wait_recv()

        @pl.when(lat > 0)
        def _():
            to_north(r).wait_recv()

    def wait_send(r):
        to_east(r).wait_send()
        to_west(r).wait_send()
        to_mirror(r).wait_send()

        @pl.when(lat > 0)
        def _():
            to_south(r).wait_send()

    for t in range(2):
        c[pl.ds(t * 8 * padded + rows, 8 * padded - rows), :] = jnp.zeros((8 * padded - rows, 128), F32)
    nf[pl.ds(rows, 8 * padded - rows), :] = jnp.zeros((8 * padded - rows, 128), F32)

    @pl.when(lat == 0)
    def _():
        s_in[...] = jnp.zeros(s_in.shape, F32)

    for load in loads[:7]:
        load.wait()
    count = jnp.where(maps[0] == 1, maps[1], 0).astype(F32)

    def prepare(k, packs):
        pt, ps, pe = packs
        drag = 1.0 / (1.0 + fields[0, at(k), :])
        e = fields[1, at(k), :] * drag
        ef[at(k), :] = e
        nf[at(k), :] = fields[2, at(k), :] * drag
        wet = k.astype(F32) < count
        x = jnp.where(wet, fields[3, at(k), :], 0.0)
        y = jnp.where(wet, fields[4, at(k), :], 0.0)
        c[at(k), :] = x
        c[at(padded + k), :] = y
        return pack(x, k, pt), pack(y, k, ps), pack(e, k, pe)

    pt, ps, pe = loop(depth, prepare, (zero, zero, zero))
    lon_out[0, 0:8, :] = pt
    lon_out[0, 8:16, :] = ps
    lon_out[0, 16:24, :] = pack(count, depth, pe)
    n_out[0, 0:8, :] = turn(jnp.broadcast_to(count[7:8, :], (8, 128)))
    s_out[0, 0:8, :] = jnp.broadcast_to(count[0:1, :], (8, 128))
    for t in range(2):
        stage_rows(0, c, t * 8 * padded, t)
    stage_rows(0, nf, 0, 2)
    pl.semaphore_wait(barrier, 3 + jnp.where(lat > 0, 1, 0))
    send_lat(0)
    send_lon(0)
    wait_recv(0)

    edges = merge(lon_w[0, 16:24, :], lon_e[0, 16:24, :])
    rim = unpack(edges, depth)
    least_w = jnp.minimum(count, jnp.where(first, rim, pltpu.roll(count, 1, 1)))
    least_e = jnp.minimum(count, jnp.where(last, rim, pltpu.roll(count, 127, 1)))
    least_s = jnp.minimum(count, jnp.where(bottom_row, s_in[0, 0:8, :], pltpu.roll(count, 1, 0)))
    least_n = jnp.minimum(count, jnp.where(top_row, n_in[0, 0:8, :], pltpu.roll(count, 7, 0)))

    def faces(k, carry):
        level = k.astype(F32)
        e, n = ef[at(k), :], nf[at(k), :]
        w = jnp.where(first, unpack(edges, k), pltpu.roll(e, 1, 1))
        s = jnp.where(bottom_row, spread(s_in, 0, 8 + 2 * padded + k), pltpu.roll(n, 1, 0))
        n = jnp.where(hinge, 0.5 * (n - spread(n_in, 0, 8 + 2 * padded + k)), n)
        oe, ow, on, os = level < least_e, level < least_w, level < least_n, level < least_s
        fe, fw = jnp.where(oe, e, 0.0), jnp.where(ow, w, 0.0)
        fn, fs = jnp.where(on, n, 0.0), jnp.where(os, s, 0.0)
        de, dw = jnp.where(oe, DIFFUSE, 0.0), jnp.where(ow, DIFFUSE, 0.0)
        dn, ds = jnp.where(on, DIFFUSE, 0.0), jnp.where(os, DIFFUSE, 0.0)
        ne, pw = de - jnp.minimum(fe, 0.0), jnp.maximum(fw, 0.0) + dw
        nn, p_s = dn - jnp.minimum(fn, 0.0), jnp.maximum(fs, 0.0) + ds
        coef[0, at(k), :] = 1.0 - ((fe + ne) + (pw - fw) + (fn + nn) + (p_s - fs))
        coef[1, at(k), :] = jnp.where(last, 0.0, ne)
        coef[2, at(k), :] = jnp.where(first, 0.0, pw)
        coef[3, at(k), :] = jnp.where(top_row, 0.0, nn)
        coef[4, at(k), :] = jnp.where(bottom_row, 0.0, p_s)
        coef[5, at(k), :] = jnp.where(first, pw, jnp.where(last, ne, 0.0))
        coef[6, at(k), :] = jnp.where(bottom_row, p_s, jnp.where(top_row, nn, 0.0))
        dv[at(k), :] = fe - fw + fn - fs
        return carry

    loop(depth, faces, 0)

    def interior():
        def body(k, carry):
            a = [coef[i, at(k), :] for i in range(5)]
            for t in range(2):
                x = c[at(t * padded + k), :]
                acc[at(t * depth + k), :] = (
                    (a[0] * x + a[1] * pltpu.roll(x, 127, 1))
                    + (a[2] * pltpu.roll(x, 1, 1) + a[3] * pltpu.roll(x, 7, 0))
                    + a[4] * pltpu.roll(x, 1, 0)
                )
            return carry

        loop(depth, body, 0)

    def completed(r, t, k, merged):
        rims = jnp.where(
            bottom_row, spread(s_in, r, 8 + t * padded + k), spread(n_in, r, 8 + t * padded + k)
        )
        return acc[at(t * depth + k), :] + (
            coef[5, at(k), :] * unpack(merged, k) + coef[6, at(k), :] * rims
        )

    def merged_of(r):
        return [
            merge(lon_w[r, 8 * t:8 * t + 8, :], lon_e[r, 8 * t:8 * t + 8, :]) for t in range(2)
        ]

    def column_bands():
        loads[7].wait()
        upp[at(0), :] = zero
        low[at(0), :] = zero
        upp[at(depth), :] = zero
        low[at(depth), :] = zero

        def deeper(i, total):
            k = depth - 1 - i
            total = total + dv[at(k), :]
            flow = -float(PASSES) * total
            mixing = jnp.where(k.astype(F32) < count, fields[5, at(k - 1), :], 0.0)
            upp[at(k), :] = jnp.maximum(flow, 0.0) + mixing
            low[at(k), :] = mixing - jnp.minimum(flow, 0.0)
            return total

        loop(depth - 1, deeper, zero)

        def pivots(k, q):
            l, u = low[at(k), :], upp[at(k + 1), :]
            inv = 1.0 / (1.0 + low[at(k + 1), :] + upp[at(k), :] - l * q)
            q = u * inv
            ip[at(k), :] = inv
            mm[at(k), :] = l * inv
            qq[at(k), :] = q
            return q

        loop(depth, pivots, zero)

    interior()
    for r in range(PASSES - 1):
        merged = merged_of(r)

        def complete(k, packs):
            new = []
            for t in range(2):
                x = completed(r, t, k, merged[t])
                c[at(t * padded + k), :] = x
                new.append(pack(x, k, packs[t]))
            return tuple(new)

        packs = loop(depth, complete, (zero, zero))
        lon_out[r + 1, 0:8, :] = packs[0]
        lon_out[r + 1, 8:16, :] = packs[1]
        for t in range(2):
            stage_rows(r + 1, c, t * 8 * padded, t)
        send_lat(r + 1)
        send_lon(r + 1)
        interior()
        if r == 0:
            column_bands()
        wait_recv(r + 1)

    merged = merged_of(PASSES - 1)

    def forward(k, values):
        new = []
        for t in range(2):
            x = completed(PASSES - 1, t, k, merged[t])
            v = x * ip[at(k), :] + mm[at(k), :] * values[t]
            res[at(t * depth + k), :] = v
            new.append(v)
        return tuple(new)

    values = loop(depth, forward, (zero, zero))

    half = depth // 2

    def backward(start):
        def body(i, values):
            k = start - i
            q = qq[at(k), :]
            new = []
            for t in range(2):
                x = res[at(t * depth + k), :] + q * values[t]
                res[at(t * depth + k), :] = x
                new.append(x)
            return tuple(new)

        return body

    stores = []

    def store(part, begin, size):
        for t, ref in enumerate((out_t, out_s)):
            copy = pltpu.make_async_copy(
                res.at[pl.ds(t * rows + begin * 8, size * 8)],
                ref.at[pl.ds(begin * 8, size * 8)],
                out_sem.at[part, t],
            )
            copy.start()
            stores.append(copy)

    values = loop(depth - half, backward(depth - 1), (zero, zero))
    store(0, half, depth - half)
    loop(half, backward(half - 1), values)
    store(1, 0, half)
    for r in range(PASSES):
        wait_send(r)
    for copy in stores:
        copy.wait()


def solution(mesh):
    nlon, nlat = mesh.shape["lon"], mesh.shape["lat"]
    cube, plane = P(None, "lat", "lon"), P("lat", "lon")

    def shards(*args):
        depth = args[0].shape[0]
        padded = -(-depth // 8) * 8
        rows = 8 * depth
        flat = [a.reshape(rows, 128) for a in args[:6]] + list(args[6:])
        edge_rows = 8 + 3 * padded
        vmem = pltpu.VMEM
        scratch = [
            vmem((6, rows, 128), F32), vmem((2, 8, 128), jnp.int32),
            vmem((16 * padded, 128), F32), vmem((2 * rows, 128), F32),
            vmem((rows, 128), F32), vmem((8 * padded, 128), F32),
            vmem((7, rows, 128), F32), vmem((rows, 128), F32),
            vmem((rows + 8, 128), F32), vmem((rows + 8, 128), F32),
            vmem((rows, 128), F32), vmem((rows, 128), F32), vmem((rows, 128), F32),
            vmem((2 * rows, 128), F32),
        ]
        scratch += [vmem((PASSES, 24, 128), F32) for _ in range(3)]
        scratch += [vmem((PASSES, edge_rows, 128), F32) for _ in range(4)]
        scratch += [
            pltpu.SemaphoreType.DMA((8,)), pltpu.SemaphoreType.DMA((PASSES, 4)),
            pltpu.SemaphoreType.DMA((PASSES, 4)), pltpu.SemaphoreType.DMA((2, 2)),
        ]
        outs = pl.pallas_call(
            functools.partial(tracer_kernel, nlon, nlat, depth),
            out_shape=[jax.ShapeDtypeStruct((rows, 128), F32)] * 2,
            in_specs=[pl.BlockSpec(memory_space=pl.ANY)] * 8,
            out_specs=[pl.BlockSpec(memory_space=pl.ANY)] * 2,
            scratch_shapes=scratch,
            compiler_params=pltpu.CompilerParams(
                collective_id=0, has_side_effects=True, vmem_limit_bytes=32 * 1024 * 1024
            ),
            cost_estimate=pl.CostEstimate(flops=20000000, bytes_accessed=1600000, transcendentals=0),
            name="tracer_step",
        )(*flat)
        return tuple(o.reshape(depth, 8, 128) for o in outs)

    return jax.shard_map(
        shards, mesh=mesh, in_specs=(cube,) * 6 + (plane,) * 2, out_specs=(cube, cube), check_vma=False
    )
```

```python
import functools

import jax
import jax.numpy as jnp
from jax import lax
from jax.experimental import pallas as pl
from jax.experimental.pallas import tpu as pltpu
from jax.sharding import PartitionSpec as P

PASSES = 4
DIFFUSE = 0.05
MESH = pl.DeviceIdType.MESH
F32 = jnp.float32


def tracer_kernel(
    nlon, nlat, depth,
    th, sa, zo, me, vd, fr, ind, dep, out_t, out_s,
    fields, maps, c, acc, ef, nf, coef, dv, upp, low, ip, mm, qq, res,
    lon_out, lon_w, lon_e, n_out, s_out, n_in, s_in,
    in_sem, send_sem, recv_sem,
):
    padded = -(-depth // 8) * 8
    rows = 8 * depth
    lon = lax.axis_index("lon")
    lat = lax.axis_index("lat")
    is_top = lat == nlat - 1
    east = lax.rem(lon + 1, nlon)
    west = lax.rem(lon + nlon - 1, nlon)
    mirror = nlon - 1 - lon

    barrier = pltpu.get_barrier_semaphore()

    def greet(i, j):
        pl.semaphore_signal(barrier, inc=1, device_id={"lon": i, "lat": j}, device_id_type=MESH)

    greet(east, lat)
    greet(west, lat)

    @pl.when(is_top)
    def _():
        greet(mirror, lat)

    @pl.when(jnp.logical_not(is_top))
    def _():
        greet(lon, lat + 1)

    @pl.when(lat > 0)
    def _():
        greet(lon, lat - 1)

    loads = [
        pltpu.make_async_copy(ind, maps.at[0], in_sem.at[0]),
        pltpu.make_async_copy(dep, maps.at[1], in_sem.at[1]),
    ]
    for f, ref in enumerate((fr, zo, me, th, sa, vd)):
        loads.append(pltpu.make_async_copy(ref, fields.at[f], in_sem.at[2 + f]))
    for load in loads:
        load.start()

    lane = lax.broadcasted_iota(jnp.int32, (8, 128), 1)
    sub = lax.broadcasted_iota(jnp.int32, (8, 128), 0)
    pair = lax.shift_right_logical(lane, 1)
    even = (lane & 1) == 0
    first, last = lane == 0, lane == 127
    bottom_row, top_row = sub == 0, sub == 7
    hinge = jnp.logical_and(top_row, is_top)
    turned = jnp.where(is_top, 127 - lane, lane)
    zero = jnp.zeros((8, 128), F32)

    def at(k):
        return pl.ds(pl.multiple_of(k * 8, 8), 8)

    def loop(count, body, init):
        return lax.fori_loop(0, count, body, init, unroll=count)

    def pack(x, k, packed):
        return jnp.where(pair == k, pltpu.roll(x, 2 * k + 1, 1), packed)

    def merge(from_west, from_east):
        return jnp.where(even, pltpu.roll(from_east, 127, 1), pltpu.roll(from_west, 1, 1))

    def unpack(merged, k):
        return pltpu.roll(merged, 127 - 2 * k, 1)

    def spread(ref, r, row):
        return jnp.broadcast_to(ref[r, pl.ds(row, 1), :], (8, 128))

    def turn(x):
        return jnp.take_along_axis(x, turned, axis=1, mode="promise_in_bounds")

    def stage_rows(r, ref, base, row):
        for j in range(padded // 8):
            place = pl.ds(row + 8 * j, 8)
            s_out[r, place, :] = ref[pl.ds(base + 64 * j, 8, stride=8), :]
            n_out[r, place, :] = turn(ref[pl.ds(base + 64 * j + 7, 8, stride=8), :])

    def copy_to(src, dst, r, g, way_out, way_in, i, j):
        return pltpu.make_async_remote_copy(
            src_ref=src, dst_ref=dst, send_sem=send_sem.at[r, g, way_out],
            recv_sem=recv_sem.at[r, g, way_in], device_id={"lon": i, "lat": j}, device_id_type=MESH,
        )

    def to_east(r, g):
        s = pl.ds(8 * g, 8)
        return copy_to(lon_out.at[r, s], lon_w.at[r, s], r, g, 0, 0, east, lat)

    def to_west(r, g):
        s = pl.ds(8 * g, 8)
        return copy_to(lon_out.at[r, s], lon_e.at[r, s], r, g, 1, 1, west, lat)

    def rows_of(g):
        return pl.ds(g * padded, padded + 8 if g == 2 else padded)

    def to_north(r, g):
        s = rows_of(g)
        return copy_to(n_out.at[r, s], s_in.at[r, s], r, g, 3, 3, lon, lat + 1)

    def to_mirror(r, g):
        s = rows_of(g)
        return copy_to(n_out.at[r, s], n_in.at[r, s], r, g, 3, 2, mirror, lat)

    def to_south(r, g):
        s = pl.ds(2 * padded, 8) if g == 2 else rows_of(g)
        return copy_to(s_out.at[r, s], n_in.at[r, s], r, g, 2, 2, lon, lat - 1)

    def send(r, g):
        @pl.when(is_top)
        def _():
            to_mirror(r, g).start()

        @pl.when(jnp.logical_not(is_top))
        def _():
            to_north(r, g).start()

        @pl.when(lat > 0)
        def _():
            to_south(r, g).start()

        to_east(r, g).start()
        to_west(r, g).start()

    def wait_recv(r, g):
        to_east(r, g).wait_recv()
        to_west(r, g).wait_recv()
        if g == 2:
            @pl.when(is_top)
            def _():
                to_mirror(r, g).wait_recv()

            @pl.when(jnp.logical_not(is_top))
            def _():
                to_south(r, g).wait_recv()
        else:
            to_south(r, g).wait_recv()

        @pl.when(lat > 0)
        def _():
            to_north(r, g).wait_recv()

    def wait_send(r, g):
        to_east(r, g).wait_send()
        to_west(r, g).wait_send()
        to_mirror(r, g).wait_send()

        @pl.when(lat > 0)
        def _():
            to_south(r, g).wait_send()

    for t in range(2):
        c[pl.ds(t * 8 * padded + rows, 8 * padded - rows), :] = jnp.zeros((8 * padded - rows, 128), F32)
    nf[pl.ds(rows, 8 * padded - rows), :] = jnp.zeros((8 * padded - rows, 128), F32)

    @pl.when(lat == 0)
    def _():
        s_in[...] = jnp.zeros(s_in.shape, F32)

    @pl.when(jnp.logical_not(is_top))
    def _():
        n_in[0, pl.ds(2 * padded + 8, padded), :] = jnp.zeros((padded, 128), F32)

    for load in loads[:5]:
        load.wait()
    count = jnp.where(maps[0] == 1, maps[1], 0).astype(F32)

    def flows(k, packed):
        drag = 1.0 / (1.0 + fields[0, at(k), :])
        e = fields[1, at(k), :] * drag
        ef[at(k), :] = e
        nf[at(k), :] = fields[2, at(k), :] * drag
        return pack(e, k, packed)

    lon_out[0, 16:24, :] = pack(count, depth, loop(depth, flows, zero))
    n_out[0, pl.ds(2 * padded, 8), :] = turn(jnp.broadcast_to(count[7:8, :], (8, 128)))
    s_out[0, pl.ds(2 * padded, 8), :] = jnp.broadcast_to(count[0:1, :], (8, 128))
    stage_rows(0, nf, 0, 2 * padded + 8)
    pl.semaphore_wait(barrier, 3 + jnp.where(lat > 0, 1, 0))
    send(0, 2)
    for t in range(2):
        loads[5 + t].wait()

        def masked(k, packed):
            x = jnp.where(k.astype(F32) < count, fields[3 + t, at(k), :], 0.0)
            c[at(t * padded + k), :] = x
            return pack(x, k, packed)

        lon_out[0, 8 * t:8 * t + 8, :] = loop(depth, masked, zero)
        stage_rows(0, c, t * 8 * padded, t * padded)
        send(0, t)
    wait_recv(0, 2)

    edges = merge(lon_w[0, 16:24, :], lon_e[0, 16:24, :])
    rim = unpack(edges, depth)
    least_w = jnp.minimum(count, jnp.where(first, rim, pltpu.roll(count, 1, 1)))
    least_e = jnp.minimum(count, jnp.where(last, rim, pltpu.roll(count, 127, 1)))
    least_s = jnp.minimum(count, jnp.where(bottom_row, s_in[0, pl.ds(2 * padded, 8), :], pltpu.roll(count, 1, 0)))
    least_n = jnp.minimum(count, jnp.where(top_row, n_in[0, pl.ds(2 * padded, 8), :], pltpu.roll(count, 7, 0)))

    def faces(k, carry):
        level = k.astype(F32)
        e, n = ef[at(k), :], nf[at(k), :]
        w = jnp.where(first, unpack(edges, k), pltpu.roll(e, 1, 1))
        s = jnp.where(bottom_row, spread(s_in, 0, 2 * padded + 8 + k), pltpu.roll(n, 1, 0))
        n = jnp.where(hinge, 0.5 * (n - spread(n_in, 0, 2 * padded + 8 + k)), n)
        oe, ow, on, os = level < least_e, level < least_w, level < least_n, level < least_s
        fe, fw = jnp.where(oe, e, 0.0), jnp.where(ow, w, 0.0)
        fn, fs = jnp.where(on, n, 0.0), jnp.where(os, s, 0.0)
        de, dw = jnp.where(oe, DIFFUSE, 0.0), jnp.where(ow, DIFFUSE, 0.0)
        dn, ds = jnp.where(on, DIFFUSE, 0.0), jnp.where(os, DIFFUSE, 0.0)
        ne, pw = de - jnp.minimum(fe, 0.0), jnp.maximum(fw, 0.0) + dw
        nn, p_s = dn - jnp.minimum(fn, 0.0), jnp.maximum(fs, 0.0) + ds
        coef[0, at(k), :] = 1.0 - ((fe + ne) + (pw - fw) + (fn + nn) + (p_s - fs))
        coef[1, at(k), :] = jnp.where(last, 0.0, ne)
        coef[2, at(k), :] = jnp.where(first, 0.0, pw)
        coef[3, at(k), :] = jnp.where(top_row, 0.0, nn)
        coef[4, at(k), :] = jnp.where(bottom_row, 0.0, p_s)
        coef[5, at(k), :] = jnp.where(first, pw, jnp.where(last, ne, 0.0))
        coef[6, at(k), :] = jnp.where(bottom_row, p_s, jnp.where(top_row, nn, 0.0))
        dv[at(k), :] = fe - fw + fn - fs
        return carry

    loop(depth, faces, 0)

    def interior(t):
        def body(k, carry):
            a = [coef[i, at(k), :] for i in range(5)]
            x = c[at(t * padded + k), :]
            acc[at(t * depth + k), :] = (
                (a[0] * x + a[1] * pltpu.roll(x, 127, 1))
                + (a[2] * pltpu.roll(x, 1, 1) + a[3] * pltpu.roll(x, 7, 0))
                + a[4] * pltpu.roll(x, 1, 0)
            )
            return carry

        loop(depth, body, 0)

    def completed(r, t, k, merged):
        rims = jnp.where(
            bottom_row, spread(s_in, r, t * padded + k), spread(n_in, r, t * padded + k)
        )
        return acc[at(t * depth + k), :] + (
            coef[5, at(k), :] * unpack(merged, k) + coef[6, at(k), :] * rims
        )

    def merged_of(r, t):
        return merge(lon_w[r, 8 * t:8 * t + 8, :], lon_e[r, 8 * t:8 * t + 8, :])

    def bands():
        loads[7].wait()
        upp[at(0), :] = zero
        low[at(0), :] = zero
        upp[at(depth), :] = zero
        low[at(depth), :] = zero

        def deeper(i, total):
            k = depth - 1 - i
            total = total + dv[at(k), :]
            flow = -float(PASSES) * total
            mixing = jnp.where(k.astype(F32) < count, fields[5, at(k - 1), :], 0.0)
            upp[at(k), :] = jnp.maximum(flow, 0.0) + mixing
            low[at(k), :] = mixing - jnp.minimum(flow, 0.0)
            return total

        loop(depth - 1, deeper, zero)

    def pivots(begin, size, q):
        def body(i, q):
            k = begin + i
            l, u = low[at(k), :], upp[at(k + 1), :]
            inv = 1.0 / (1.0 + low[at(k + 1), :] + upp[at(k), :] - l * q)
            q = u * inv
            ip[at(k), :] = inv
            mm[at(k), :] = l * inv
            qq[at(k), :] = q
            return q

        return loop(size, body, q)

    half = depth // 2
    interior(0)
    interior(1)
    for r in range(PASSES - 1):
        for t in range(2):
            wait_recv(r, t)
            merged = merged_of(r, t)

            def complete(k, packed):
                x = completed(r, t, k, merged)
                c[at(t * padded + k), :] = x
                return pack(x, k, packed)

            lon_out[r + 1, 8 * t:8 * t + 8, :] = loop(depth, complete, zero)
            stage_rows(r + 1, c, t * 8 * padded, t * padded)
            send(r + 1, t)
        interior(0)
        interior(1)
        if r == 0:
            bands()
        elif r == 1:
            q = pivots(0, half, zero)
        else:
            pivots(half, depth - half, q)

    merged = []
    for t in range(2):
        wait_recv(PASSES - 1, t)
        merged.append(merged_of(PASSES - 1, t))

    def forward(k, values):
        new = []
        for t in range(2):
            x = completed(PASSES - 1, t, k, merged[t])
            v = x * ip[at(k), :] + mm[at(k), :] * values[t]
            res[at(t * depth + k), :] = v
            new.append(v)
        return tuple(new)

    values = loop(depth, forward, (zero, zero))

    def backward(i, values):
        k = depth - 1 - i
        q = qq[at(k), :]
        new = []
        for t, out in enumerate((out_t, out_s)):
            x = res[at(t * depth + k), :] + q * values[t]
            out[at(k), :] = x
            new.append(x)
        return tuple(new)

    loop(depth, backward, (zero, zero))
    for r in range(PASSES):
        for g in range(3 if r == 0 else 2):
            wait_send(r, g)


def solution(mesh):
    nlon, nlat = mesh.shape["lon"], mesh.shape["lat"]
    cube, plane = P(None, "lat", "lon"), P("lat", "lon")

    def shards(*args):
        depth = args[0].shape[0]
        padded = -(-depth // 8) * 8
        rows = 8 * depth
        flat = [a.reshape(rows, 128) for a in args[:6]] + list(args[6:])
        edge_rows = 8 + 3 * padded
        vmem = pltpu.VMEM
        scratch = [
            vmem((6, rows, 128), F32), vmem((2, 8, 128), jnp.int32),
            vmem((16 * padded, 128), F32), vmem((2 * rows, 128), F32),
            vmem((rows, 128), F32), vmem((8 * padded, 128), F32),
            vmem((7, rows, 128), F32), vmem((rows, 128), F32),
            vmem((rows + 8, 128), F32), vmem((rows + 8, 128), F32),
            vmem((rows, 128), F32), vmem((rows, 128), F32), vmem((rows, 128), F32),
            vmem((2 * rows, 128), F32),
        ]
        scratch += [vmem((PASSES, 24, 128), F32) for _ in range(3)]
        scratch += [vmem((PASSES, edge_rows, 128), F32) for _ in range(4)]
        scratch += [
            pltpu.SemaphoreType.DMA((8,)), pltpu.SemaphoreType.DMA((PASSES, 3, 4)),
            pltpu.SemaphoreType.DMA((PASSES, 3, 4)),
        ]
        outs = pl.pallas_call(
            functools.partial(tracer_kernel, nlon, nlat, depth),
            out_shape=[jax.ShapeDtypeStruct((rows, 128), F32)] * 2,
            in_specs=[pl.BlockSpec(memory_space=pltpu.HBM)] * 8,
            out_specs=[pl.BlockSpec(memory_space=pltpu.VMEM)] * 2,
            scratch_shapes=scratch,
            compiler_params=pltpu.CompilerParams(
                collective_id=0, has_side_effects=True, vmem_limit_bytes=56 * 1024 * 1024
            ),
            cost_estimate=pl.CostEstimate(flops=20000000, bytes_accessed=1600000, transcendentals=0),
            name="tracer_step",
        )(*flat)
        return tuple(o.reshape(depth, 8, 128) for o in outs)

    return jax.shard_map(
        shards, mesh=mesh, in_specs=(cube,) * 6 + (plane,) * 2, out_specs=(cube, cube), check_vma=False
    )
```

```python
import functools

import jax
import jax.numpy as jnp
from jax import lax
from jax.experimental import pallas as pl
from jax.experimental.pallas import tpu as pltpu
from jax.sharding import PartitionSpec as P

PASSES = 4
DIFFUSE = 0.05
MESH = pl.DeviceIdType.MESH
F32 = jnp.float32


def tracer_kernel(
    nlon, nlat, depth,
    th, sa, zo, me, vd, fr, ind, dep, out_t, out_s,
    fields, maps, c, acc, ef, nf, coef, dv, upp, low, ip, mm, qq, res,
    lon_out, lon_w, lon_e, n_out, s_out, n_in, s_in,
    in_sem, send_sem, recv_sem,
):
    padded = -(-depth // 8) * 8
    rows = 8 * depth
    lon = lax.axis_index("lon")
    lat = lax.axis_index("lat")
    is_top = lat == nlat - 1
    part = -(-depth // 2)
    east = lax.rem(lon + 1, nlon)
    west = lax.rem(lon + nlon - 1, nlon)
    mirror = nlon - 1 - lon

    barrier = pltpu.get_barrier_semaphore()

    def greet(i, j):
        pl.semaphore_signal(barrier, inc=1, device_id={"lon": i, "lat": j}, device_id_type=MESH)

    greet(east, lat)
    greet(west, lat)

    @pl.when(is_top)
    def _():
        greet(mirror, lat)

    @pl.when(jnp.logical_not(is_top))
    def _():
        greet(lon, lat + 1)

    @pl.when(lat > 0)
    def _():
        greet(lon, lat - 1)

    loads = [
        pltpu.make_async_copy(ind, maps.at[0], in_sem.at[0]),
        pltpu.make_async_copy(dep, maps.at[1], in_sem.at[1]),
    ]
    for f, ref in enumerate((fr, zo, me, th, sa, vd)):
        loads.append(pltpu.make_async_copy(ref, fields.at[f], in_sem.at[2 + f]))
    for load in loads:
        load.start()

    lane = lax.broadcasted_iota(jnp.int32, (8, 128), 1)
    sub = lax.broadcasted_iota(jnp.int32, (8, 128), 0)
    pair = lax.shift_right_logical(lane, 1)
    even = (lane & 1) == 0
    first, last = lane == 0, lane == 127
    bottom_row, top_row = sub == 0, sub == 7
    hinge = jnp.logical_and(top_row, is_top)
    turned = jnp.where(is_top, 127 - lane, lane)
    zero = jnp.zeros((8, 128), F32)

    def at(k):
        return pl.ds(pl.multiple_of(k * 8, 8), 8)

    def loop(count, body, init, unroll=None):
        return lax.fori_loop(0, count, body, init, unroll=count if unroll is None else unroll)

    def pack(x, k, packed):
        return jnp.where(pair == k, pltpu.roll(x, 2 * k + 1, 1), packed)

    def merge(from_west, from_east):
        return jnp.where(even, pltpu.roll(from_east, 127, 1), pltpu.roll(from_west, 1, 1))

    def unpack(merged, k):
        return pltpu.roll(merged, 127 - 2 * k, 1)

    def spread(ref, r, row):
        return jnp.broadcast_to(ref[r, pl.ds(row, 1), :], (8, 128))

    def turn(x):
        return jnp.take_along_axis(x, turned, axis=1, mode="promise_in_bounds")

    def stage_rows(r, ref, base, row):
        for j in range(padded // 8):
            place = pl.ds(row + 8 * j, 8)
            s_out[r, place, :] = ref[pl.ds(base + 64 * j, 8, stride=8), :]
            n_out[r, place, :] = turn(ref[pl.ds(base + 64 * j + 7, 8, stride=8), :])

    def copy_to(src, dst, r, g, way_out, way_in, i, j):
        return pltpu.make_async_remote_copy(
            src_ref=src, dst_ref=dst, send_sem=send_sem.at[r, g, way_out],
            recv_sem=recv_sem.at[r, g, way_in], device_id={"lon": i, "lat": j}, device_id_type=MESH,
        )

    def to_east(r, g):
        s = pl.ds(8 * g, 8)
        return copy_to(lon_out.at[r, s], lon_w.at[r, s], r, g, 0, 0, east, lat)

    def to_west(r, g):
        s = pl.ds(8 * g, 8)
        return copy_to(lon_out.at[r, s], lon_e.at[r, s], r, g, 1, 1, west, lat)

    def rows_of(g):
        return pl.ds(g * padded, padded + 8 if g == 2 else padded)

    def to_north(r, g):
        s = rows_of(g)
        return copy_to(n_out.at[r, s], s_in.at[r, s], r, g, 3, 3, lon, lat + 1)

    def to_mirror(r, g):
        s = rows_of(g)
        return copy_to(n_out.at[r, s], n_in.at[r, s], r, g, 3, 2, mirror, lat)

    def to_south(r, g):
        s = pl.ds(2 * padded, 8) if g == 2 else rows_of(g)
        return copy_to(s_out.at[r, s], n_in.at[r, s], r, g, 2, 2, lon, lat - 1)

    def send(r, g):
        @pl.when(is_top)
        def _():
            to_mirror(r, g).start()

        @pl.when(jnp.logical_not(is_top))
        def _():
            to_north(r, g).start()

        @pl.when(lat > 0)
        def _():
            to_south(r, g).start()

        to_east(r, g).start()
        to_west(r, g).start()

    def wait_recv(r, g):
        to_east(r, g).wait_recv()
        to_west(r, g).wait_recv()
        if g == 2:
            @pl.when(is_top)
            def _():
                to_mirror(r, g).wait_recv()

            @pl.when(jnp.logical_not(is_top))
            def _():
                to_south(r, g).wait_recv()
        else:
            to_south(r, g).wait_recv()

        @pl.when(lat > 0)
        def _():
            to_north(r, g).wait_recv()

    def wait_send(r, g):
        to_east(r, g).wait_send()
        to_west(r, g).wait_send()
        to_mirror(r, g).wait_send()

        @pl.when(lat > 0)
        def _():
            to_south(r, g).wait_send()

    for t in range(2):
        c[pl.ds(t * 8 * padded + rows, 8 * padded - rows), :] = jnp.zeros((8 * padded - rows, 128), F32)
    nf[pl.ds(rows, 8 * padded - rows), :] = jnp.zeros((8 * padded - rows, 128), F32)

    @pl.when(lat == 0)
    def _():
        s_in[...] = jnp.zeros(s_in.shape, F32)

    @pl.when(jnp.logical_not(is_top))
    def _():
        n_in[0, pl.ds(2 * padded + 8, padded), :] = jnp.zeros((padded, 128), F32)

    for load in loads[:5]:
        load.wait()
    count = jnp.where(maps[0] == 1, maps[1], 0).astype(F32)

    def flows(k, packed):
        drag = 1.0 / (1.0 + fields[0, at(k), :])
        e = fields[1, at(k), :] * drag
        ef[at(k), :] = e
        nf[at(k), :] = fields[2, at(k), :] * drag
        return pack(e, k, packed)

    lon_out[0, 16:24, :] = pack(count, depth, loop(depth, flows, zero, part))
    n_out[0, pl.ds(2 * padded, 8), :] = turn(jnp.broadcast_to(count[7:8, :], (8, 128)))
    s_out[0, pl.ds(2 * padded, 8), :] = jnp.broadcast_to(count[0:1, :], (8, 128))
    stage_rows(0, nf, 0, 2 * padded + 8)
    pl.semaphore_wait(barrier, 3 + jnp.where(lat > 0, 1, 0))
    send(0, 2)
    for t in range(2):
        loads[5 + t].wait()

        def masked(k, packed):
            x = jnp.where(k.astype(F32) < count, fields[3 + t, at(k), :], 0.0)
            c[at(t * padded + k), :] = x
            return pack(x, k, packed)

        lon_out[0, 8 * t:8 * t + 8, :] = loop(depth, masked, zero)
        stage_rows(0, c, t * 8 * padded, t * padded)
        send(0, t)
    wait_recv(0, 2)

    edges = merge(lon_w[0, 16:24, :], lon_e[0, 16:24, :])
    rim = unpack(edges, depth)
    least_w = jnp.minimum(count, jnp.where(first, rim, pltpu.roll(count, 1, 1)))
    least_e = jnp.minimum(count, jnp.where(last, rim, pltpu.roll(count, 127, 1)))
    least_s = jnp.minimum(count, jnp.where(bottom_row, s_in[0, pl.ds(2 * padded, 8), :], pltpu.roll(count, 1, 0)))
    least_n = jnp.minimum(count, jnp.where(top_row, n_in[0, pl.ds(2 * padded, 8), :], pltpu.roll(count, 7, 0)))

    def faces(k, carry):
        level = k.astype(F32)
        e, n = ef[at(k), :], nf[at(k), :]
        w = jnp.where(first, unpack(edges, k), pltpu.roll(e, 1, 1))
        s = jnp.where(bottom_row, spread(s_in, 0, 2 * padded + 8 + k), pltpu.roll(n, 1, 0))
        n = jnp.where(hinge, 0.5 * (n - spread(n_in, 0, 2 * padded + 8 + k)), n)
        oe, ow, on, os = level < least_e, level < least_w, level < least_n, level < least_s
        fe, fw = jnp.where(oe, e, 0.0), jnp.where(ow, w, 0.0)
        fn, fs = jnp.where(on, n, 0.0), jnp.where(os, s, 0.0)
        de, dw = jnp.where(oe, DIFFUSE, 0.0), jnp.where(ow, DIFFUSE, 0.0)
        dn, ds = jnp.where(on, DIFFUSE, 0.0), jnp.where(os, DIFFUSE, 0.0)
        ne, pw = de - jnp.minimum(fe, 0.0), jnp.maximum(fw, 0.0) + dw
        nn, p_s = dn - jnp.minimum(fn, 0.0), jnp.maximum(fs, 0.0) + ds
        coef[0, at(k), :] = 1.0 - ((fe + ne) + (pw - fw) + (fn + nn) + (p_s - fs))
        coef[1, at(k), :] = jnp.where(last, 0.0, ne)
        coef[2, at(k), :] = jnp.where(first, 0.0, pw)
        coef[3, at(k), :] = jnp.where(top_row, 0.0, nn)
        coef[4, at(k), :] = jnp.where(bottom_row, 0.0, p_s)
        coef[5, at(k), :] = jnp.where(first, pw, jnp.where(last, ne, 0.0))
        coef[6, at(k), :] = jnp.where(bottom_row, p_s, jnp.where(top_row, nn, 0.0))
        dv[at(k), :] = fe - fw + fn - fs
        return carry

    loop(depth, faces, 0, part)

    def interior(t):
        def body(k, carry):
            a = [coef[i, at(k), :] for i in range(5)]
            x = c[at(t * padded + k), :]
            acc[at(t * depth + k), :] = (
                (a[0] * x + a[1] * pltpu.roll(x, 127, 1))
                + (a[2] * pltpu.roll(x, 1, 1) + a[3] * pltpu.roll(x, 7, 0))
                + a[4] * pltpu.roll(x, 1, 0)
            )
            return carry

        loop(depth, body, 0)

    def completed(r, t, k, merged):
        rims = jnp.where(
            bottom_row, spread(s_in, r, t * padded + k), spread(n_in, r, t * padded + k)
        )
        return acc[at(t * depth + k), :] + (
            coef[5, at(k), :] * unpack(merged, k) + coef[6, at(k), :] * rims
        )

    def merged_of(r, t):
        return merge(lon_w[r, 8 * t:8 * t + 8, :], lon_e[r, 8 * t:8 * t + 8, :])

    def bands():
        loads[7].wait()
        upp[at(0), :] = zero
        low[at(0), :] = zero
        upp[at(depth), :] = zero
        low[at(depth), :] = zero

        def deeper(i, total):
            k = depth - 1 - i
            total = total + dv[at(k), :]
            flow = -float(PASSES) * total
            mixing = jnp.where(k.astype(F32) < count, fields[5, at(k - 1), :], 0.0)
            upp[at(k), :] = jnp.maximum(flow, 0.0) + mixing
            low[at(k), :] = mixing - jnp.minimum(flow, 0.0)
            return total

        loop(depth - 1, deeper, zero, 5)

    def pivots(begin, size):
        q = qq[at(jnp.int32(begin - 1)), :] if begin else zero

        def body(i, q):
            k = begin + i
            l, u = low[at(k), :], upp[at(k + 1), :]
            inv = 1.0 / (1.0 + low[at(k + 1), :] + upp[at(k), :] - l * q)
            q = u * inv
            ip[at(k), :] = inv
            mm[at(k), :] = l * inv
            qq[at(k), :] = q
            return q

        loop(size, body, q, 4)

    half = depth // 2
    wait_send(0, 2)

    def substep(r, carry):
        interior(0)
        interior(1)
        pl.when(r == 0)(bands)
        pl.when(r == 1)(lambda: pivots(0, half))
        pl.when(r == 2)(lambda: pivots(half, depth - half))
        for t in range(2):
            wait_send(r, t)
            wait_recv(r, t)
            merged = merged_of(r, t)

            def complete(k, packed):
                x = completed(r, t, k, merged)
                c[at(t * padded + k), :] = x
                return pack(x, k, packed)

            lon_out[r + 1, 8 * t:8 * t + 8, :] = loop(depth, complete, zero)
            stage_rows(r + 1, c, t * 8 * padded, t * padded)
            send(r + 1, t)
        return carry

    lax.fori_loop(0, PASSES - 1, substep, 0)
    interior(0)
    interior(1)

    merged = []
    for t in range(2):
        wait_recv(PASSES - 1, t)
        merged.append(merged_of(PASSES - 1, t))

    def forward(k, values):
        new = []
        for t in range(2):
            x = completed(PASSES - 1, t, k, merged[t])
            v = x * ip[at(k), :] + mm[at(k), :] * values[t]
            res[at(t * depth + k), :] = v
            new.append(v)
        return tuple(new)

    values = loop(depth, forward, (zero, zero))

    def backward(i, values):
        k = depth - 1 - i
        q = qq[at(k), :]
        new = []
        for t, out in enumerate((out_t, out_s)):
            x = res[at(t * depth + k), :] + q * values[t]
            out[at(k), :] = x
            new.append(x)
        return tuple(new)

    loop(depth, backward, (zero, zero))
    for t in range(2):
        wait_send(PASSES - 1, t)


def solution(mesh):
    nlon, nlat = mesh.shape["lon"], mesh.shape["lat"]
    cube, plane = P(None, "lat", "lon"), P("lat", "lon")

    def shards(*args):
        depth = args[0].shape[0]
        padded = -(-depth // 8) * 8
        rows = 8 * depth
        flat = [a.reshape(rows, 128) for a in args[:6]] + list(args[6:])
        edge_rows = 8 + 3 * padded
        vmem = pltpu.VMEM
        scratch = [
            vmem((6, rows, 128), F32), vmem((2, 8, 128), jnp.int32),
            vmem((16 * padded, 128), F32), vmem((2 * rows, 128), F32),
            vmem((rows, 128), F32), vmem((8 * padded, 128), F32),
            vmem((7, rows, 128), F32), vmem((rows, 128), F32),
            vmem((rows + 8, 128), F32), vmem((rows + 8, 128), F32),
            vmem((rows, 128), F32), vmem((rows, 128), F32), vmem((rows, 128), F32),
            vmem((2 * rows, 128), F32),
        ]
        scratch += [vmem((PASSES, 24, 128), F32) for _ in range(3)]
        scratch += [vmem((PASSES, edge_rows, 128), F32) for _ in range(4)]
        scratch += [
            pltpu.SemaphoreType.DMA((8,)), pltpu.SemaphoreType.DMA((PASSES, 3, 4)),
            pltpu.SemaphoreType.DMA((PASSES, 3, 4)),
        ]
        outs = pl.pallas_call(
            functools.partial(tracer_kernel, nlon, nlat, depth),
            out_shape=[jax.ShapeDtypeStruct((rows, 128), F32)] * 2,
            in_specs=[pl.BlockSpec(memory_space=pltpu.HBM)] * 8,
            out_specs=[pl.BlockSpec(memory_space=pltpu.VMEM)] * 2,
            scratch_shapes=scratch,
            compiler_params=pltpu.CompilerParams(
                collective_id=0, has_side_effects=True, vmem_limit_bytes=54784 * 1024
            ),
            cost_estimate=pl.CostEstimate(flops=20000000, bytes_accessed=1600000, transcendentals=0),
            name="tracer_step",
        )(*flat)
        return tuple(o.reshape(depth, 8, 128) for o in outs)

    return jax.shard_map(
        shards, mesh=mesh, in_specs=(cube,) * 6 + (plane,) * 2, out_specs=(cube, cube), check_vma=False
    )
```

```python
import functools

import jax
import jax.numpy as jnp
from jax import lax
from jax.experimental import pallas as pl
from jax.experimental.pallas import tpu as pltpu
from jax.sharding import PartitionSpec as P

PASSES = 4
DIFFUSE = 0.05
MESH = pl.DeviceIdType.MESH
F32 = jnp.float32


def tracer_kernel(
    nlon, nlat, depth,
    th, sa, zo, me, vd, fr, ind, dep, out_t, out_s,
    fields, maps, c, acc, ef, nf, coef, dv, upp, low, ip, mm, qq, res,
    lon_out, lon_w, lon_e, n_out, s_out, n_in, s_in,
    in_sem, send_sem, recv_sem,
):
    padded = -(-depth // 8) * 8
    rows = 8 * depth
    lon = lax.axis_index("lon")
    lat = lax.axis_index("lat")
    is_top = lat == nlat - 1
    part = -(-depth // 2)
    east = lax.rem(lon + 1, nlon)
    west = lax.rem(lon + nlon - 1, nlon)
    mirror = nlon - 1 - lon

    barrier = pltpu.get_barrier_semaphore()

    def greet(i, j):
        pl.semaphore_signal(barrier, inc=1, device_id={"lon": i, "lat": j}, device_id_type=MESH)

    greet(east, lat)
    greet(west, lat)

    @pl.when(is_top)
    def _():
        greet(mirror, lat)

    @pl.when(jnp.logical_not(is_top))
    def _():
        greet(lon, lat + 1)

    @pl.when(lat > 0)
    def _():
        greet(lon, lat - 1)

    loads = [
        pltpu.make_async_copy(ind, maps.at[0], in_sem.at[0]),
        pltpu.make_async_copy(dep, maps.at[1], in_sem.at[1]),
    ]
    for f, ref in enumerate((fr, zo, me, th, sa, vd)):
        loads.append(pltpu.make_async_copy(ref, fields.at[f], in_sem.at[2 + f]))
    for load in loads:
        load.start()

    lane = lax.broadcasted_iota(jnp.int32, (8, 128), 1)
    sub = lax.broadcasted_iota(jnp.int32, (8, 128), 0)
    pair = lax.shift_right_logical(lane, 1)
    even = (lane & 1) == 0
    first, last = lane == 0, lane == 127
    bottom_row, top_row = sub == 0, sub == 7
    hinge = jnp.logical_and(top_row, is_top)
    turned = jnp.where(is_top, 127 - lane, lane)
    zero = jnp.zeros((8, 128), F32)

    def at(k):
        return pl.ds(pl.multiple_of(k * 8, 8), 8)

    def loop(count, body, init, unroll=None):
        return lax.fori_loop(0, count, body, init, unroll=count if unroll is None else unroll)

    def pack(x, k, packed):
        return jnp.where(pair == k, pltpu.roll(x, 2 * k + 1, 1), packed)

    def merge(from_west, from_east):
        return jnp.where(even, pltpu.roll(from_east, 127, 1), pltpu.roll(from_west, 1, 1))

    def unpack(merged, k):
        return pltpu.roll(merged, 127 - 2 * k, 1)

    def spread(ref, r, row):
        return jnp.broadcast_to(ref[r, pl.ds(row, 1), :], (8, 128))

    def turn(x):
        return jnp.take_along_axis(x, turned, axis=1, mode="promise_in_bounds")

    def stage_rows(r, ref, base, row):
        for j in range(padded // 8):
            place = pl.ds(row + 8 * j, 8)
            s_out[r, place, :] = ref[pl.ds(base + 64 * j, 8, stride=8), :]
            n_out[r, place, :] = turn(ref[pl.ds(base + 64 * j + 7, 8, stride=8), :])

    def copy_to(src, dst, r, g, way_out, way_in, i, j):
        return pltpu.make_async_remote_copy(
            src_ref=src, dst_ref=dst, send_sem=send_sem.at[r, g, way_out],
            recv_sem=recv_sem.at[r, g, way_in], device_id={"lon": i, "lat": j}, device_id_type=MESH,
        )

    def to_east(r, g):
        s = pl.ds(8 * g, 8)
        return copy_to(lon_out.at[r, s], lon_w.at[r, s], r, g, 0, 0, east, lat)

    def to_west(r, g):
        s = pl.ds(8 * g, 8)
        return copy_to(lon_out.at[r, s], lon_e.at[r, s], r, g, 1, 1, west, lat)

    def rows_of(g):
        return pl.ds(g * padded, padded + 8 if g == 2 else padded)

    def to_north(r, g):
        s = rows_of(g)
        return copy_to(n_out.at[r, s], s_in.at[r, s], r, g, 3, 3, lon, lat + 1)

    def to_mirror(r, g):
        s = rows_of(g)
        return copy_to(n_out.at[r, s], n_in.at[r, s], r, g, 3, 2, mirror, lat)

    def to_south(r, g):
        s = pl.ds(2 * padded, 8) if g == 2 else rows_of(g)
        return copy_to(s_out.at[r, s], n_in.at[r, s], r, g, 2, 2, lon, lat - 1)

    def send(r, g):
        @pl.when(is_top)
        def _():
            to_mirror(r, g).start()

        @pl.when(jnp.logical_not(is_top))
        def _():
            to_north(r, g).start()

        @pl.when(lat > 0)
        def _():
            to_south(r, g).start()

        to_east(r, g).start()
        to_west(r, g).start()

    def wait_recv(r, g):
        to_east(r, g).wait_recv()
        to_west(r, g).wait_recv()
        if g == 2:
            @pl.when(is_top)
            def _():
                to_mirror(r, g).wait_recv()

            @pl.when(jnp.logical_not(is_top))
            def _():
                to_south(r, g).wait_recv()
        else:
            to_south(r, g).wait_recv()

        @pl.when(lat > 0)
        def _():
            to_north(r, g).wait_recv()

    def wait_send(r, g):
        to_east(r, g).wait_send()
        to_west(r, g).wait_send()
        to_mirror(r, g).wait_send()

        @pl.when(lat > 0)
        def _():
            to_south(r, g).wait_send()

    for t in range(2):
        c[pl.ds(t * 8 * padded + rows, 8 * padded - rows), :] = jnp.zeros((8 * padded - rows, 128), F32)
    nf[pl.ds(rows, 8 * padded - rows), :] = jnp.zeros((8 * padded - rows, 128), F32)

    @pl.when(lat == 0)
    def _():
        s_in[...] = jnp.zeros(s_in.shape, F32)

    @pl.when(jnp.logical_not(is_top))
    def _():
        n_in[0, pl.ds(2 * padded + 8, padded), :] = jnp.zeros((padded, 128), F32)

    for load in loads[:5]:
        load.wait()
    count = jnp.where(maps[0] == 1, maps[1], 0).astype(F32)

    def flows(k, packed):
        drag = 1.0 / (1.0 + fields[0, at(k), :])
        e = fields[1, at(k), :] * drag
        ef[at(k), :] = e
        nf[at(k), :] = fields[2, at(k), :] * drag
        return pack(e, k, packed)

    lon_out[0, 16:24, :] = pack(count, depth, loop(depth, flows, zero, part))
    n_out[0, pl.ds(2 * padded, 8), :] = turn(jnp.broadcast_to(count[7:8, :], (8, 128)))
    s_out[0, pl.ds(2 * padded, 8), :] = jnp.broadcast_to(count[0:1, :], (8, 128))
    stage_rows(0, nf, 0, 2 * padded + 8)
    pl.semaphore_wait(barrier, 3 + jnp.where(lat > 0, 1, 0))
    send(0, 2)
    for t in range(2):
        loads[5 + t].wait()

        def masked(k, packed):
            x = jnp.where(k.astype(F32) < count, fields[3 + t, at(k), :], 0.0)
            c[at(t * padded + k), :] = x
            return pack(x, k, packed)

        lon_out[0, 8 * t:8 * t + 8, :] = loop(depth, masked, zero)
        stage_rows(0, c, t * 8 * padded, t * padded)
        send(0, t)
    wait_recv(0, 2)

    edges = merge(lon_w[0, 16:24, :], lon_e[0, 16:24, :])
    rim = unpack(edges, depth)
    least_w = jnp.minimum(count, jnp.where(first, rim, pltpu.roll(count, 1, 1)))
    least_e = jnp.minimum(count, jnp.where(last, rim, pltpu.roll(count, 127, 1)))
    least_s = jnp.minimum(count, jnp.where(bottom_row, s_in[0, pl.ds(2 * padded, 8), :], pltpu.roll(count, 1, 0)))
    least_n = jnp.minimum(count, jnp.where(top_row, n_in[0, pl.ds(2 * padded, 8), :], pltpu.roll(count, 7, 0)))

    def inside(a, t, k):
        x = c[at(t * padded + k), :]
        acc[at(t * depth + k), :] = (
            (a[0] * x + a[1] * pltpu.roll(x, 127, 1))
            + (a[2] * pltpu.roll(x, 1, 1) + a[3] * pltpu.roll(x, 7, 0))
            + a[4] * pltpu.roll(x, 1, 0)
        )

    def faces(k, carry):
        level = k.astype(F32)
        e, n = ef[at(k), :], nf[at(k), :]
        w = jnp.where(first, unpack(edges, k), pltpu.roll(e, 1, 1))
        s = jnp.where(bottom_row, spread(s_in, 0, 2 * padded + 8 + k), pltpu.roll(n, 1, 0))
        n = jnp.where(hinge, 0.5 * (n - spread(n_in, 0, 2 * padded + 8 + k)), n)
        oe, ow, on, os = level < least_e, level < least_w, level < least_n, level < least_s
        fe, fw = jnp.where(oe, e, 0.0), jnp.where(ow, w, 0.0)
        fn, fs = jnp.where(on, n, 0.0), jnp.where(os, s, 0.0)
        de, dw = jnp.where(oe, DIFFUSE, 0.0), jnp.where(ow, DIFFUSE, 0.0)
        dn, ds = jnp.where(on, DIFFUSE, 0.0), jnp.where(os, DIFFUSE, 0.0)
        ne, pw = de - jnp.minimum(fe, 0.0), jnp.maximum(fw, 0.0) + dw
        nn, p_s = dn - jnp.minimum(fn, 0.0), jnp.maximum(fs, 0.0) + ds
        a = (
            1.0 - ((fe + ne) + (pw - fw) + (fn + nn) + (p_s - fs)),
            jnp.where(last, 0.0, ne),
            jnp.where(first, 0.0, pw),
            jnp.where(top_row, 0.0, nn),
            jnp.where(bottom_row, 0.0, p_s),
        )
        for i, values in enumerate(a):
            coef[i, at(k), :] = values
        for t in range(2):
            inside(a, t, k)
        coef[5, at(k), :] = jnp.where(first, pw, jnp.where(last, ne, 0.0))
        coef[6, at(k), :] = jnp.where(bottom_row, p_s, jnp.where(top_row, nn, 0.0))
        dv[at(k), :] = fe - fw + fn - fs
        return carry

    loop(depth, faces, 0, part)

    def interior(t):
        def body(k, carry):
            inside([coef[i, at(k), :] for i in range(5)], t, k)
            return carry

        loop(depth, body, 0)

    def completed(r, t, k, merged):
        rims = jnp.where(
            bottom_row, spread(s_in, r, t * padded + k), spread(n_in, r, t * padded + k)
        )
        return acc[at(t * depth + k), :] + (
            coef[5, at(k), :] * unpack(merged, k) + coef[6, at(k), :] * rims
        )

    def merged_of(r, t):
        return merge(lon_w[r, 8 * t:8 * t + 8, :], lon_e[r, 8 * t:8 * t + 8, :])

    def bands():
        loads[7].wait()
        upp[at(0), :] = zero
        low[at(0), :] = zero
        upp[at(depth), :] = zero
        low[at(depth), :] = zero

        def deeper(i, total):
            k = depth - 1 - i
            total = total + dv[at(k), :]
            flow = -float(PASSES) * total
            mixing = jnp.where(k.astype(F32) < count, fields[5, at(k - 1), :], 0.0)
            upp[at(k), :] = jnp.maximum(flow, 0.0) + mixing
            low[at(k), :] = mixing - jnp.minimum(flow, 0.0)
            return total

        loop(depth - 1, deeper, zero, 5)

    def pivots(begin, size):
        q = qq[at(jnp.int32(begin - 1)), :] if begin else zero

        def body(i, q):
            k = begin + i
            l, u = low[at(k), :], upp[at(k + 1), :]
            inv = 1.0 / (1.0 + low[at(k + 1), :] + upp[at(k), :] - l * q)
            q = u * inv
            ip[at(k), :] = inv
            mm[at(k), :] = l * inv
            qq[at(k), :] = q
            return q

        loop(size, body, q, 4)

    half = depth // 2
    wait_send(0, 2)

    def substep(r, carry):
        for t in range(2):
            wait_send(r, t)
            wait_recv(r, t)
            merged = merged_of(r, t)

            def complete(k, packed):
                x = completed(r, t, k, merged)
                c[at(t * padded + k), :] = x
                return pack(x, k, packed)

            lon_out[r + 1, 8 * t:8 * t + 8, :] = loop(depth, complete, zero)
            stage_rows(r + 1, c, t * 8 * padded, t * padded)
            send(r + 1, t)
        interior(0)
        interior(1)
        pl.when(r == 0)(bands)
        pl.when(r == 1)(lambda: pivots(0, half))
        pl.when(r == 2)(lambda: pivots(half, depth - half))
        return carry

    lax.fori_loop(0, PASSES - 1, substep, 0)

    merged = []
    for t in range(2):
        wait_recv(PASSES - 1, t)
        merged.append(merged_of(PASSES - 1, t))

    def forward(k, values):
        new = []
        for t in range(2):
            x = completed(PASSES - 1, t, k, merged[t])
            v = x * ip[at(k), :] + mm[at(k), :] * values[t]
            res[at(t * depth + k), :] = v
            new.append(v)
        return tuple(new)

    values = loop(depth, forward, (zero, zero))

    def backward(i, values):
        k = depth - 1 - i
        q = qq[at(k), :]
        new = []
        for t, out in enumerate((out_t, out_s)):
            x = res[at(t * depth + k), :] + q * values[t]
            out[at(k), :] = x
            new.append(x)
        return tuple(new)

    loop(depth, backward, (zero, zero))
    for t in range(2):
        wait_send(PASSES - 1, t)


def solution(mesh):
    nlon, nlat = mesh.shape["lon"], mesh.shape["lat"]
    cube, plane = P(None, "lat", "lon"), P("lat", "lon")

    def shards(*args):
        depth = args[0].shape[0]
        padded = -(-depth // 8) * 8
        rows = 8 * depth
        flat = [a.reshape(rows, 128) for a in args[:6]] + list(args[6:])
        edge_rows = 8 + 3 * padded
        vmem = pltpu.VMEM
        scratch = [
            vmem((6, rows, 128), F32), vmem((2, 8, 128), jnp.int32),
            vmem((16 * padded, 128), F32), vmem((2 * rows, 128), F32),
            vmem((rows, 128), F32), vmem((8 * padded, 128), F32),
            vmem((7, rows, 128), F32), vmem((rows, 128), F32),
            vmem((rows + 8, 128), F32), vmem((rows + 8, 128), F32),
            vmem((rows, 128), F32), vmem((rows, 128), F32), vmem((rows, 128), F32),
            vmem((2 * rows, 128), F32),
        ]
        scratch += [vmem((PASSES, 24, 128), F32) for _ in range(3)]
        scratch += [vmem((PASSES, edge_rows, 128), F32) for _ in range(4)]
        scratch += [
            pltpu.SemaphoreType.DMA((8,)), pltpu.SemaphoreType.DMA((PASSES, 3, 4)),
            pltpu.SemaphoreType.DMA((PASSES, 3, 4)),
        ]
        outs = pl.pallas_call(
            functools.partial(tracer_kernel, nlon, nlat, depth),
            out_shape=[jax.ShapeDtypeStruct((rows, 128), F32)] * 2,
            in_specs=[pl.BlockSpec(memory_space=pltpu.HBM)] * 8,
            out_specs=[pl.BlockSpec(memory_space=pltpu.VMEM)] * 2,
            scratch_shapes=scratch,
            compiler_params=pltpu.CompilerParams(
                collective_id=0, has_side_effects=True, vmem_limit_bytes=54784 * 1024
            ),
            cost_estimate=pl.CostEstimate(flops=20000000, bytes_accessed=1600000, transcendentals=0),
            name="tracer_step",
        )(*flat)
        return tuple(o.reshape(depth, 8, 128) for o in outs)

    return jax.shard_map(
        shards, mesh=mesh, in_specs=(cube,) * 6 + (plane,) * 2, out_specs=(cube, cube), check_vma=False
    )
```

```python
import functools

import jax
import jax.numpy as jnp
from jax import lax
from jax.experimental import pallas as pl
from jax.experimental.pallas import tpu as pltpu
from jax.sharding import PartitionSpec as P

PASSES = 4
DIFFUSE = 0.05
MESH = pl.DeviceIdType.MESH
F32 = jnp.float32


def tracer_kernel(
    nlon, nlat, depth,
    th, sa, zo, me, vd, fr, ind, dep, out_t, out_s,
    fields, maps, c, acc, ef, nf, coef, dv, upp, low, ip, mm, qq, res,
    lon_out, lon_w, lon_e, n_out, s_out, n_in, s_in,
    in_sem, send_sem, recv_sem,
):
    padded = -(-depth // 8) * 8
    rows = 8 * depth
    lon = lax.axis_index("lon")
    lat = lax.axis_index("lat")
    is_top = lat == nlat - 1
    part = -(-depth // 2)
    east = lax.rem(lon + 1, nlon)
    west = lax.rem(lon + nlon - 1, nlon)
    mirror = nlon - 1 - lon

    barrier = pltpu.get_barrier_semaphore()

    def greet(i, j):
        pl.semaphore_signal(barrier, inc=1, device_id={"lon": i, "lat": j}, device_id_type=MESH)

    greet(east, lat)
    greet(west, lat)

    @pl.when(is_top)
    def _():
        greet(mirror, lat)

    @pl.when(jnp.logical_not(is_top))
    def _():
        greet(lon, lat + 1)

    @pl.when(lat > 0)
    def _():
        greet(lon, lat - 1)

    loads = [
        pltpu.make_async_copy(ind, maps.at[0], in_sem.at[0]),
        pltpu.make_async_copy(dep, maps.at[1], in_sem.at[1]),
    ]
    for f, ref in enumerate((fr, zo, me, th, sa, vd)):
        loads.append(pltpu.make_async_copy(ref, fields.at[f], in_sem.at[2 + f]))
    for load in loads:
        load.start()

    lane = lax.broadcasted_iota(jnp.int32, (8, 128), 1)
    sub = lax.broadcasted_iota(jnp.int32, (8, 128), 0)
    pair = lax.shift_right_logical(lane, 1)
    even = (lane & 1) == 0
    first, last = lane == 0, lane == 127
    bottom_row, top_row = sub == 0, sub == 7
    hinge = jnp.logical_and(top_row, is_top)
    turned = jnp.where(is_top, 127 - lane, lane)
    zero = jnp.zeros((8, 128), F32)

    def at(k):
        return pl.ds(pl.multiple_of(k * 8, 8), 8)

    def loop(count, body, init, unroll=None):
        return lax.fori_loop(0, count, body, init, unroll=count if unroll is None else unroll)

    def pack(x, k, packed):
        return jnp.where(pair == k, pltpu.roll(x, 2 * k + 1, 1), packed)

    def merge(from_west, from_east):
        return jnp.where(even, pltpu.roll(from_east, 127, 1), pltpu.roll(from_west, 1, 1))

    def unpack(merged, k):
        return pltpu.roll(merged, 127 - 2 * k, 1)

    def spread(ref, r, row):
        return jnp.broadcast_to(ref[r, pl.ds(row, 1), :], (8, 128))

    def turn(x):
        return jnp.take_along_axis(x, turned, axis=1, mode="promise_in_bounds")

    def stage_rows(r, ref, base, row):
        for j in range(padded // 8):
            place = pl.ds(row + 8 * j, 8)
            s_out[r, place, :] = ref[pl.ds(base + 64 * j, 8, stride=8), :]
            n_out[r, place, :] = turn(ref[pl.ds(base + 64 * j + 7, 8, stride=8), :])

    def copy_to(src, dst, r, g, way_out, way_in, i, j):
        return pltpu.make_async_remote_copy(
            src_ref=src, dst_ref=dst, send_sem=send_sem.at[r, g, way_out],
            recv_sem=recv_sem.at[r, g, way_in], device_id={"lon": i, "lat": j}, device_id_type=MESH,
        )

    def to_east(r, g):
        s = pl.ds(8 * g, 8)
        return copy_to(lon_out.at[r, s], lon_w.at[r, s], r, g, 0, 0, east, lat)

    def to_west(r, g):
        s = pl.ds(8 * g, 8)
        return copy_to(lon_out.at[r, s], lon_e.at[r, s], r, g, 1, 1, west, lat)

    def rows_of(g):
        return pl.ds(g * padded, padded + 8 if g == 2 else padded)

    def to_north(r, g):
        s = rows_of(g)
        return copy_to(n_out.at[r, s], s_in.at[r, s], r, g, 3, 3, lon, lat + 1)

    def to_mirror(r, g):
        s = rows_of(g)
        return copy_to(n_out.at[r, s], n_in.at[r, s], r, g, 3, 2, mirror, lat)

    def to_south(r, g):
        s = pl.ds(2 * padded, 8) if g == 2 else rows_of(g)
        return copy_to(s_out.at[r, s], n_in.at[r, s], r, g, 2, 2, lon, lat - 1)

    def send(r, g):
        @pl.when(is_top)
        def _():
            to_mirror(r, g).start()

        @pl.when(jnp.logical_not(is_top))
        def _():
            to_north(r, g).start()

        @pl.when(lat > 0)
        def _():
            to_south(r, g).start()

    def send_sides(r, g):
        to_east(r, g).start()
        to_west(r, g).start()

    def wait_recv(r, g):
        to_east(r, g).wait_recv()
        to_west(r, g).wait_recv()
        if g == 2:
            @pl.when(is_top)
            def _():
                to_mirror(r, g).wait_recv()

            @pl.when(jnp.logical_not(is_top))
            def _():
                to_south(r, g).wait_recv()
        else:
            to_south(r, g).wait_recv()

        @pl.when(lat > 0)
        def _():
            to_north(r, g).wait_recv()

    def wait_send(r, g):
        to_east(r, g).wait_send()
        to_west(r, g).wait_send()
        to_mirror(r, g).wait_send()

        @pl.when(lat > 0)
        def _():
            to_south(r, g).wait_send()

    for t in range(2):
        c[pl.ds(t * 8 * padded + rows, 8 * padded - rows), :] = jnp.zeros((8 * padded - rows, 128), F32)
    nf[pl.ds(rows, 8 * padded - rows), :] = jnp.zeros((8 * padded - rows, 128), F32)

    @pl.when(lat == 0)
    def _():
        s_in[...] = jnp.zeros(s_in.shape, F32)

    @pl.when(jnp.logical_not(is_top))
    def _():
        n_in[0, pl.ds(2 * padded + 8, padded), :] = jnp.zeros((padded, 128), F32)

    for load in loads[:5]:
        load.wait()
    count = jnp.where(maps[0] == 1, maps[1], 0).astype(F32)

    def flows(k, packed):
        drag = 1.0 / (1.0 + fields[0, at(k), :])
        e = fields[1, at(k), :] * drag
        ef[at(k), :] = e
        nf[at(k), :] = fields[2, at(k), :] * drag
        return pack(e, k, packed)

    lon_out[0, 16:24, :] = pack(count, depth, loop(depth, flows, zero, part))
    n_out[0, pl.ds(2 * padded, 8), :] = turn(jnp.broadcast_to(count[7:8, :], (8, 128)))
    s_out[0, pl.ds(2 * padded, 8), :] = jnp.broadcast_to(count[0:1, :], (8, 128))
    stage_rows(0, nf, 0, 2 * padded + 8)
    pl.semaphore_wait(barrier, 3 + jnp.where(lat > 0, 1, 0))
    send_sides(0, 2)
    send(0, 2)
    for t in range(2):
        loads[5 + t].wait()

        def masked(k, packed):
            x = jnp.where(k.astype(F32) < count, fields[3 + t, at(k), :], 0.0)
            c[at(t * padded + k), :] = x
            return pack(x, k, packed)

        lon_out[0, 8 * t:8 * t + 8, :] = loop(depth, masked, zero)
        send_sides(0, t)
        stage_rows(0, c, t * 8 * padded, t * padded)
        send(0, t)
    wait_recv(0, 2)

    edges = merge(lon_w[0, 16:24, :], lon_e[0, 16:24, :])
    rim = unpack(edges, depth)
    least_w = jnp.minimum(count, jnp.where(first, rim, pltpu.roll(count, 1, 1)))
    least_e = jnp.minimum(count, jnp.where(last, rim, pltpu.roll(count, 127, 1)))
    least_s = jnp.minimum(count, jnp.where(bottom_row, s_in[0, pl.ds(2 * padded, 8), :], pltpu.roll(count, 1, 0)))
    least_n = jnp.minimum(count, jnp.where(top_row, n_in[0, pl.ds(2 * padded, 8), :], pltpu.roll(count, 7, 0)))

    def inside(a, t, k):
        x = c[at(t * padded + k), :]
        acc[at(t * depth + k), :] = (
            (a[0] * x + a[1] * pltpu.roll(x, 127, 1))
            + (a[2] * pltpu.roll(x, 1, 1) + a[3] * pltpu.roll(x, 7, 0))
            + a[4] * pltpu.roll(x, 1, 0)
        )

    def faces(k, carry):
        level = k.astype(F32)
        e, n = ef[at(k), :], nf[at(k), :]
        w = jnp.where(first, unpack(edges, k), pltpu.roll(e, 1, 1))
        s = jnp.where(bottom_row, spread(s_in, 0, 2 * padded + 8 + k), pltpu.roll(n, 1, 0))
        n = jnp.where(hinge, 0.5 * (n - spread(n_in, 0, 2 * padded + 8 + k)), n)
        oe, ow, on, os = level < least_e, level < least_w, level < least_n, level < least_s
        fe, fw = jnp.where(oe, e, 0.0), jnp.where(ow, w, 0.0)
        fn, fs = jnp.where(on, n, 0.0), jnp.where(os, s, 0.0)
        de, dw = jnp.where(oe, DIFFUSE, 0.0), jnp.where(ow, DIFFUSE, 0.0)
        dn, ds = jnp.where(on, DIFFUSE, 0.0), jnp.where(os, DIFFUSE, 0.0)
        ne, pw = de - jnp.minimum(fe, 0.0), jnp.maximum(fw, 0.0) + dw
        nn, p_s = dn - jnp.minimum(fn, 0.0), jnp.maximum(fs, 0.0) + ds
        a = (
            1.0 - ((fe + ne) + (pw - fw) + (fn + nn) + (p_s - fs)),
            jnp.where(last, 0.0, ne),
            jnp.where(first, 0.0, pw),
            jnp.where(top_row, 0.0, nn),
            jnp.where(bottom_row, 0.0, p_s),
        )
        for i, values in enumerate(a):
            coef[i, at(k), :] = values
        for t in range(2):
            inside(a, t, k)
        coef[5, at(k), :] = jnp.where(first, pw, jnp.where(last, ne, 0.0))
        coef[6, at(k), :] = jnp.where(bottom_row, p_s, jnp.where(top_row, nn, 0.0))
        dv[at(k), :] = fe - fw + fn - fs
        return carry

    loop(depth, faces, 0, part)

    def interior(t):
        def body(k, carry):
            inside([coef[i, at(k), :] for i in range(5)], t, k)
            return carry

        loop(depth, body, 0)

    def completed(r, t, k, merged):
        rims = jnp.where(
            bottom_row, spread(s_in, r, t * padded + k), spread(n_in, r, t * padded + k)
        )
        return acc[at(t * depth + k), :] + (
            coef[5, at(k), :] * unpack(merged, k) + coef[6, at(k), :] * rims
        )

    def merged_of(r, t):
        return merge(lon_w[r, 8 * t:8 * t + 8, :], lon_e[r, 8 * t:8 * t + 8, :])

    def bands():
        loads[7].wait()
        upp[at(0), :] = zero
        low[at(0), :] = zero
        upp[at(depth), :] = zero
        low[at(depth), :] = zero

        def deeper(i, total):
            k = depth - 1 - i
            total = total + dv[at(k), :]
            flow = -float(PASSES) * total
            mixing = jnp.where(k.astype(F32) < count, fields[5, at(k - 1), :], 0.0)
            upp[at(k), :] = jnp.maximum(flow, 0.0) + mixing
            low[at(k), :] = mixing - jnp.minimum(flow, 0.0)
            return total

        loop(depth - 1, deeper, zero, 5)

    def pivots(begin, size):
        q = qq[at(jnp.int32(begin - 1)), :] if begin else zero

        def body(i, q):
            k = begin + i
            l, u = low[at(k), :], upp[at(k + 1), :]
            inv = 1.0 / (1.0 + low[at(k + 1), :] + upp[at(k), :] - l * q)
            q = u * inv
            ip[at(k), :] = inv
            mm[at(k), :] = l * inv
            qq[at(k), :] = q
            return q

        loop(size, body, q, 4)

    half = depth // 2
    wait_send(0, 2)

    def substep(r, carry):
        for t in range(2):
            wait_send(r, t)
            wait_recv(r, t)
            merged = merged_of(r, t)

            def complete(k, packed):
                x = completed(r, t, k, merged)
                c[at(t * padded + k), :] = x
                return pack(x, k, packed)

            lon_out[r + 1, 8 * t:8 * t + 8, :] = loop(depth, complete, zero)
            send_sides(r + 1, t)
            stage_rows(r + 1, c, t * 8 * padded, t * padded)
            send(r + 1, t)
        interior(0)
        interior(1)
        pl.when(r == 0)(bands)
        pl.when(r == 1)(lambda: pivots(0, half))
        pl.when(r == 2)(lambda: pivots(half, depth - half))
        return carry

    lax.fori_loop(0, PASSES - 1, substep, 0)

    merged = []
    for t in range(2):
        wait_recv(PASSES - 1, t)
        merged.append(merged_of(PASSES - 1, t))

    def forward(k, values):
        new = []
        for t in range(2):
            x = completed(PASSES - 1, t, k, merged[t])
            v = x * ip[at(k), :] + mm[at(k), :] * values[t]
            res[at(t * depth + k), :] = v
            new.append(v)
        return tuple(new)

    values = loop(depth, forward, (zero, zero))

    def backward(i, values):
        k = depth - 1 - i
        q = qq[at(k), :]
        new = []
        for t, out in enumerate((out_t, out_s)):
            x = res[at(t * depth + k), :] + q * values[t]
            out[at(k), :] = x
            new.append(x)
        return tuple(new)

    loop(depth, backward, (zero, zero))
    for t in range(2):
        wait_send(PASSES - 1, t)


def solution(mesh):
    nlon, nlat = mesh.shape["lon"], mesh.shape["lat"]
    cube, plane = P(None, "lat", "lon"), P("lat", "lon")

    def shards(*args):
        depth = args[0].shape[0]
        padded = -(-depth // 8) * 8
        rows = 8 * depth
        flat = [a.reshape(rows, 128) for a in args[:6]] + list(args[6:])
        edge_rows = 8 + 3 * padded
        vmem = pltpu.VMEM
        scratch = [
            vmem((6, rows, 128), F32), vmem((2, 8, 128), jnp.int32),
            vmem((16 * padded, 128), F32), vmem((2 * rows, 128), F32),
            vmem((rows, 128), F32), vmem((8 * padded, 128), F32),
            vmem((7, rows, 128), F32), vmem((rows, 128), F32),
            vmem((rows + 8, 128), F32), vmem((rows + 8, 128), F32),
            vmem((rows, 128), F32), vmem((rows, 128), F32), vmem((rows, 128), F32),
            vmem((2 * rows, 128), F32),
        ]
        scratch += [vmem((PASSES, 24, 128), F32) for _ in range(3)]
        scratch += [vmem((PASSES, edge_rows, 128), F32) for _ in range(4)]
        scratch += [
            pltpu.SemaphoreType.DMA((8,)), pltpu.SemaphoreType.DMA((PASSES, 3, 4)),
            pltpu.SemaphoreType.DMA((PASSES, 3, 4)),
        ]
        outs = pl.pallas_call(
            functools.partial(tracer_kernel, nlon, nlat, depth),
            out_shape=[jax.ShapeDtypeStruct((rows, 128), F32)] * 2,
            in_specs=[pl.BlockSpec(memory_space=pltpu.HBM)] * 8,
            out_specs=[pl.BlockSpec(memory_space=pltpu.VMEM)] * 2,
            scratch_shapes=scratch,
            compiler_params=pltpu.CompilerParams(
                collective_id=0, has_side_effects=True, vmem_limit_bytes=54784 * 1024
            ),
            cost_estimate=pl.CostEstimate(flops=20000000, bytes_accessed=1600000, transcendentals=0),
            name="tracer_step",
        )(*flat)
        return tuple(o.reshape(depth, 8, 128) for o in outs)

    return jax.shard_map(
        shards, mesh=mesh, in_specs=(cube,) * 6 + (plane,) * 2, out_specs=(cube, cube), check_vma=False
    )
```

```python
import functools

import jax
import jax.numpy as jnp
from jax import lax
from jax.experimental import pallas as pl
from jax.experimental.pallas import tpu as pltpu
from jax.sharding import PartitionSpec as P

PASSES = 4
DIFFUSE = 0.05
MESH = pl.DeviceIdType.MESH
F32 = jnp.float32


def tracer_kernel(
    nlon, nlat, depth,
    th, sa, zo, me, vd, fr, ind, dep, out_t, out_s,
    fields, maps, c, acc, ef, nf, coef, dv, upp, low, ip, mm, qq, res,
    lon_out, lon_w, lon_e, n_out, s_out, n_in, s_in,
    in_sem, send_sem, recv_sem,
):
    padded = -(-depth // 8) * 8
    rows = 8 * depth
    lon = lax.axis_index("lon")
    lat = lax.axis_index("lat")
    is_top = lat == nlat - 1
    part = -(-depth // 2)
    east = lax.rem(lon + 1, nlon)
    west = lax.rem(lon + nlon - 1, nlon)
    mirror = nlon - 1 - lon

    barrier = pltpu.get_barrier_semaphore()

    def greet(i, j):
        pl.semaphore_signal(barrier, inc=1, device_id={"lon": i, "lat": j}, device_id_type=MESH)

    greet(east, lat)
    greet(west, lat)

    @pl.when(is_top)
    def _():
        greet(mirror, lat)

    @pl.when(jnp.logical_not(is_top))
    def _():
        greet(lon, lat + 1)

    @pl.when(lat > 0)
    def _():
        greet(lon, lat - 1)

    loads = [
        pltpu.make_async_copy(ind, maps.at[0], in_sem.at[0]),
        pltpu.make_async_copy(dep, maps.at[1], in_sem.at[1]),
    ]
    for f, ref in enumerate((fr, zo, me, th, sa, vd)):
        loads.append(pltpu.make_async_copy(ref, fields.at[f], in_sem.at[2 + f]))
    for load in loads:
        load.start()

    lane = lax.broadcasted_iota(jnp.int32, (8, 128), 1)
    sub = lax.broadcasted_iota(jnp.int32, (8, 128), 0)
    pair = lax.shift_right_logical(lane, 1)
    even = (lane & 1) == 0
    first, last = lane == 0, lane == 127
    bottom_row, top_row = sub == 0, sub == 7
    hinge = jnp.logical_and(top_row, is_top)
    turned = jnp.where(is_top, 127 - lane, lane)
    zero = jnp.zeros((8, 128), F32)

    def at(k):
        return pl.ds(pl.multiple_of(k * 8, 8), 8)

    def loop(count, body, init, unroll=None):
        return lax.fori_loop(0, count, body, init, unroll=count if unroll is None else unroll)

    def pack(x, k, packed):
        return jnp.where(pair == k, pltpu.roll(x, 2 * k + 1, 1), packed)

    def merge(from_west, from_east):
        return jnp.where(even, pltpu.roll(from_east, 127, 1), pltpu.roll(from_west, 1, 1))

    def unpack(merged, k):
        return pltpu.roll(merged, 127 - 2 * k, 1)

    def spread(ref, r, row):
        return jnp.broadcast_to(ref[r, pl.ds(row, 1), :], (8, 128))

    def turn(x):
        return jnp.take_along_axis(x, turned, axis=1, mode="promise_in_bounds")

    def stage_rows(r, ref, base, row):
        for j in range(padded // 8):
            place = pl.ds(row + 8 * j, 8)
            s_out[r, place, :] = ref[pl.ds(base + 64 * j, 8, stride=8), :]
            n_out[r, place, :] = turn(ref[pl.ds(base + 64 * j + 7, 8, stride=8), :])

    def copy_to(src, dst, r, g, way_out, way_in, i, j):
        return pltpu.make_async_remote_copy(
            src_ref=src, dst_ref=dst, send_sem=send_sem.at[r, g, way_out],
            recv_sem=recv_sem.at[r, g, way_in], device_id={"lon": i, "lat": j}, device_id_type=MESH,
        )

    def to_east(r, g):
        s = pl.ds(8 * g, 8)
        return copy_to(lon_out.at[r, s], lon_w.at[r, s], r, g, 0, 0, east, lat)

    def to_west(r, g):
        s = pl.ds(8 * g, 8)
        return copy_to(lon_out.at[r, s], lon_e.at[r, s], r, g, 1, 1, west, lat)

    def rows_of(g):
        return pl.ds(g * padded, padded + 8 if g == 2 else padded)

    def to_north(r, g):
        s = rows_of(g)
        return copy_to(n_out.at[r, s], s_in.at[r, s], r, g, 3, 3, lon, lat + 1)

    def to_mirror(r, g):
        s = rows_of(g)
        return copy_to(n_out.at[r, s], n_in.at[r, s], r, g, 3, 2, mirror, lat)

    def to_south(r, g):
        s = pl.ds(2 * padded, 8) if g == 2 else rows_of(g)
        return copy_to(s_out.at[r, s], n_in.at[r, s], r, g, 2, 2, lon, lat - 1)

    def send(r, g):
        @pl.when(is_top)
        def _():
            to_mirror(r, g).start()

        @pl.when(jnp.logical_not(is_top))
        def _():
            to_north(r, g).start()

        @pl.when(lat > 0)
        def _():
            to_south(r, g).start()

        to_east(r, g).start()
        to_west(r, g).start()

    def wait_recv(r, g):
        to_east(r, g).wait_recv()
        to_west(r, g).wait_recv()
        if g == 2:
            @pl.when(is_top)
            def _():
                to_mirror(r, g).wait_recv()

            @pl.when(jnp.logical_not(is_top))
            def _():
                to_south(r, g).wait_recv()
        else:
            to_south(r, g).wait_recv()

        @pl.when(lat > 0)
        def _():
            to_north(r, g).wait_recv()

    def wait_send(r, g):
        to_east(r, g).wait_send()
        to_west(r, g).wait_send()
        to_mirror(r, g).wait_send()

        @pl.when(lat > 0)
        def _():
            to_south(r, g).wait_send()

    for t in range(2):
        c[pl.ds(t * 8 * padded + rows, 8 * padded - rows), :] = jnp.zeros((8 * padded - rows, 128), F32)
    nf[pl.ds(rows, 8 * padded - rows), :] = jnp.zeros((8 * padded - rows, 128), F32)

    @pl.when(lat == 0)
    def _():
        s_in[...] = jnp.zeros(s_in.shape, F32)

    @pl.when(jnp.logical_not(is_top))
    def _():
        n_in[0, pl.ds(2 * padded + 8, padded), :] = jnp.zeros((padded, 128), F32)

    for load in loads[:5]:
        load.wait()
    count = jnp.where(maps[0] == 1, maps[1], 0).astype(F32)

    def flows(k, packed):
        drag = 1.0 / (1.0 + fields[0, at(k), :])
        e = fields[1, at(k), :] * drag
        ef[at(k), :] = e
        nf[at(k), :] = fields[2, at(k), :] * drag
        return pack(e, k, packed)

    lon_out[0, 16:24, :] = pack(count, depth, loop(depth, flows, zero, part))
    n_out[0, pl.ds(2 * padded, 8), :] = turn(jnp.broadcast_to(count[7:8, :], (8, 128)))
    s_out[0, pl.ds(2 * padded, 8), :] = jnp.broadcast_to(count[0:1, :], (8, 128))
    stage_rows(0, nf, 0, 2 * padded + 8)
    pl.semaphore_wait(barrier, 3 + jnp.where(lat > 0, 1, 0))
    send(0, 2)
    for t in range(2):
        loads[5 + t].wait()

        def masked(k, packed):
            x = jnp.where(k.astype(F32) < count, fields[3 + t, at(k), :], 0.0)
            c[at(t * padded + k), :] = x
            return pack(x, k, packed)

        lon_out[0, 8 * t:8 * t + 8, :] = loop(depth, masked, zero)
        stage_rows(0, c, t * 8 * padded, t * padded)
        send(0, t)
    wait_recv(0, 2)

    edges = merge(lon_w[0, 16:24, :], lon_e[0, 16:24, :])
    rim = unpack(edges, depth)
    least_w = jnp.minimum(count, jnp.where(first, rim, pltpu.roll(count, 1, 1)))
    least_e = jnp.minimum(count, jnp.where(last, rim, pltpu.roll(count, 127, 1)))
    least_s = jnp.minimum(count, jnp.where(bottom_row, s_in[0, pl.ds(2 * padded, 8), :], pltpu.roll(count, 1, 0)))
    least_n = jnp.minimum(count, jnp.where(top_row, n_in[0, pl.ds(2 * padded, 8), :], pltpu.roll(count, 7, 0)))

    def inside(a, t, k):
        x = c[at(t * padded + k), :]
        acc[at(t * depth + k), :] = (
            (a[0] * x + a[1] * pltpu.roll(x, 127, 1))
            + (a[2] * pltpu.roll(x, 1, 1) + a[3] * pltpu.roll(x, 7, 0))
            + a[4] * pltpu.roll(x, 1, 0)
        )

    def faces(k, carry):
        level = k.astype(F32)
        e, n = ef[at(k), :], nf[at(k), :]
        w = jnp.where(first, unpack(edges, k), pltpu.roll(e, 1, 1))
        s = jnp.where(bottom_row, spread(s_in, 0, 2 * padded + 8 + k), pltpu.roll(n, 1, 0))
        n = jnp.where(hinge, 0.5 * (n - spread(n_in, 0, 2 * padded + 8 + k)), n)
        oe, ow, on, os = level < least_e, level < least_w, level < least_n, level < least_s
        fe, fw = jnp.where(oe, e, 0.0), jnp.where(ow, w, 0.0)
        fn, fs = jnp.where(on, n, 0.0), jnp.where(os, s, 0.0)
        de, dw = jnp.where(oe, DIFFUSE, 0.0), jnp.where(ow, DIFFUSE, 0.0)
        dn, ds = jnp.where(on, DIFFUSE, 0.0), jnp.where(os, DIFFUSE, 0.0)
        ne, pw = de - jnp.minimum(fe, 0.0), jnp.maximum(fw, 0.0) + dw
        nn, p_s = dn - jnp.minimum(fn, 0.0), jnp.maximum(fs, 0.0) + ds
        a = (
            1.0 - ((fe + ne) + (pw - fw) + (fn + nn) + (p_s - fs)),
            jnp.where(last, 0.0, ne),
            jnp.where(first, 0.0, pw),
            jnp.where(top_row, 0.0, nn),
            jnp.where(bottom_row, 0.0, p_s),
        )
        for i, values in enumerate(a):
            coef[i, at(k), :] = values
        for t in range(2):
            inside(a, t, k)
        coef[5, at(k), :] = jnp.where(first, pw, jnp.where(last, ne, 0.0))
        coef[6, at(k), :] = jnp.where(bottom_row, p_s, jnp.where(top_row, nn, 0.0))
        dv[at(k), :] = fe - fw + fn - fs
        return carry

    loop(depth, faces, 0, part)

    def interior(t):
        def body(k, carry):
            inside([coef[i, at(k), :] for i in range(5)], t, k)
            return carry

        loop(depth, body, 0)

    def completed(r, t, k, merged):
        rims = jnp.where(
            bottom_row, spread(s_in, r, t * padded + k), spread(n_in, r, t * padded + k)
        )
        return acc[at(t * depth + k), :] + (
            coef[5, at(k), :] * unpack(merged, k) + coef[6, at(k), :] * rims
        )

    def merged_of(r, t):
        return merge(lon_w[r, 8 * t:8 * t + 8, :], lon_e[r, 8 * t:8 * t + 8, :])

    def bands():
        loads[7].wait()
        upp[at(0), :] = zero
        low[at(0), :] = zero
        upp[at(depth), :] = zero
        low[at(depth), :] = zero

        def deeper(i, total):
            k = depth - 1 - i
            total = total + dv[at(k), :]
            flow = -float(PASSES) * total
            mixing = jnp.where(k.astype(F32) < count, fields[5, at(k - 1), :], 0.0)
            upp[at(k), :] = jnp.maximum(flow, 0.0) + mixing
            low[at(k), :] = mixing - jnp.minimum(flow, 0.0)
            return total

        loop(depth - 1, deeper, zero, 5)

    def pivots(begin, size):
        q = qq[at(jnp.int32(begin - 1)), :] if begin else zero

        def body(i, q):
            k = begin + i
            l, u = low[at(k), :], upp[at(k + 1), :]
            inv = 1.0 / (1.0 + low[at(k + 1), :] + upp[at(k), :] - l * q)
            q = u * inv
            ip[at(k), :] = inv
            mm[at(k), :] = l * inv
            qq[at(k), :] = q
            return q

        loop(size, body, q, 4)

    half = depth // 2
    wait_send(0, 2)

    def substep(r, carry):
        for t in range(2):
            wait_send(r, t)
            wait_recv(r, t)
            merged = merged_of(r, t)

            def complete(k, packed):
                x = completed(r, t, k, merged)
                c[at(t * padded + k), :] = x
                return pack(x, k, packed)

            lon_out[r + 1, 8 * t:8 * t + 8, :] = loop(depth, complete, zero)
            stage_rows(r + 1, c, t * 8 * padded, t * padded)
            send(r + 1, t)
        interior(0)
        interior(1)
        pl.when(r == 0)(bands)
        pl.when(r == 1)(lambda: pivots(0, half))
        pl.when(r == 2)(lambda: pivots(half, depth - half))
        return carry

    lax.fori_loop(0, PASSES - 1, substep, 0)

    for t in range(2):
        wait_recv(PASSES - 1, t)
        merged = merged_of(PASSES - 1, t)

        def forward(k, value):
            x = completed(PASSES - 1, t, k, merged)
            v = x * ip[at(k), :] + mm[at(k), :] * value
            res[at(t * depth + k), :] = v
            return v

        loop(depth, forward, zero)

    def backward(i, values):
        k = depth - 1 - i
        q = qq[at(k), :]
        new = []
        for t, out in enumerate((out_t, out_s)):
            x = res[at(t * depth + k), :] + q * values[t]
            out[at(k), :] = x
            new.append(x)
        return tuple(new)

    loop(depth, backward, (zero, zero))
    for t in range(2):
        wait_send(PASSES - 1, t)


def solution(mesh):
    nlon, nlat = mesh.shape["lon"], mesh.shape["lat"]
    cube, plane = P(None, "lat", "lon"), P("lat", "lon")

    def shards(*args):
        depth = args[0].shape[0]
        padded = -(-depth // 8) * 8
        rows = 8 * depth
        flat = [a.reshape(rows, 128) for a in args[:6]] + list(args[6:])
        edge_rows = 8 + 3 * padded
        vmem = pltpu.VMEM
        scratch = [
            vmem((6, rows, 128), F32), vmem((2, 8, 128), jnp.int32),
            vmem((16 * padded, 128), F32), vmem((2 * rows, 128), F32),
            vmem((rows, 128), F32), vmem((8 * padded, 128), F32),
            vmem((7, rows, 128), F32), vmem((rows, 128), F32),
            vmem((rows + 8, 128), F32), vmem((rows + 8, 128), F32),
            vmem((rows, 128), F32), vmem((rows, 128), F32), vmem((rows, 128), F32),
            vmem((2 * rows, 128), F32),
        ]
        scratch += [vmem((PASSES, 24, 128), F32) for _ in range(3)]
        scratch += [vmem((PASSES, edge_rows, 128), F32) for _ in range(4)]
        scratch += [
            pltpu.SemaphoreType.DMA((8,)), pltpu.SemaphoreType.DMA((PASSES, 3, 4)),
            pltpu.SemaphoreType.DMA((PASSES, 3, 4)),
        ]
        outs = pl.pallas_call(
            functools.partial(tracer_kernel, nlon, nlat, depth),
            out_shape=[jax.ShapeDtypeStruct((rows, 128), F32)] * 2,
            in_specs=[pl.BlockSpec(memory_space=pltpu.HBM)] * 8,
            out_specs=[pl.BlockSpec(memory_space=pltpu.VMEM)] * 2,
            scratch_shapes=scratch,
            compiler_params=pltpu.CompilerParams(
                collective_id=0, has_side_effects=True, vmem_limit_bytes=54784 * 1024
            ),
            cost_estimate=pl.CostEstimate(flops=20000000, bytes_accessed=1600000, transcendentals=0),
            name="tracer_step",
        )(*flat)
        return tuple(o.reshape(depth, 8, 128) for o in outs)

    return jax.shard_map(
        shards, mesh=mesh, in_specs=(cube,) * 6 + (plane,) * 2, out_specs=(cube, cube), check_vma=False
    )
```
